256 devices in a mesh: blk: 128 (over z, x, y), rhs: 2 (over core).
Axes of the slice: x: 4, y: 4, z: 8, core: 2. Of those that a mesh axis runs over, the one named last changes fastest.
Arguments:
- right_side: float32 [1024, 128, 128], P('blk', 'rhs'), may hold values from -8.4 to 8.4
- diag_tiles: bfloat16 [1024, 128, 128], P('blk'), may hold values from -0.085 to 1.33, as said below
- cond_tiles: bfloat16 [1024, 8, 128, 128], P('blk', 'rhs'), may hold values from -0.046875 to 0.046875
- neighbour_blocks: int32 [1024, 8], P('blk'), may hold values from 0 to 1023, as said below
- precision_diag: float32 [1024, 128], P('blk'), may hold values from 0.5 to 2
- precond_tiles: bfloat16 [1024, 128, 128], P('blk'), may hold values from -0.08 to 2.08, as said below
Outputs:
- solution: float32 [1024, 128, 128], P('blk', 'rhs')
- residual: float32 [1024, 128, 128], P('blk', 'rhs')
The draws below stay inside these ranges and needn't reach their ends.
Inputs may be any that keep to these rules, and one draw needn't show every extreme that they name: `neighbour_blocks`: device d holds blocks 8 * d to 8 * d + 7. No block names itself; every block names exactly 7 blocks held by other devices, and the lists of one device's blocks name blocks of any one other device at most 1 times in all, a bound that is reached. `diag_tiles`: each tile has a positive diagonal. `precond_tiles`: each tile is symmetric with a positive diagonal.
All inputs are finite; a program needn't handle non-finite values.
Results may differ from the reference program's by a relative error of at most 0.0003.
Values may be sent and summed in bfloat16 or wider, within the bound.
No kernel may reach another device: no remote copies, remote signals or barrier semaphores. Data moves between devices by JAX's collectives and lax.ppermute only.
A program may use at most 128 MiB of HBM per device.

```python
import math
import jax
import jax.numpy as jnp
from jax import lax

BS = 128
K = 8
REMOTE = 7
NRHS = 128
ITERS = 3
BLK_DEV = 8
NB = 1024


def draw_neighbour_blocks(key, part):
    key = jax.random.fold_in(key, 11)
    node_count = NB // BLK_DEV
    first_key, second_key, third_key, fourth_key = jax.random.split(key, 4)
    block_range = jnp.arange(BLK_DEV, dtype=jnp.int32)
    node_range = jnp.arange(node_count, dtype=jnp.int32)
    offsets = jax.random.randint(first_key, (node_count, BLK_DEV, K - REMOTE), 0, BLK_DEV - 1)
    local_pick = (block_range[None, :, None] + 1 + offsets) % BLK_DEV
    local_global = node_range[:, None, None] * BLK_DEV + local_pick
    orders = jax.vmap(lambda single: jax.random.permutation(single, REMOTE * BLK_DEV))(jax.random.split(second_key, node_count))
    residues = orders % (node_count - 1) * (node_count // 2 - 1) % (node_count - 1)
    peers = (node_range[:, None] + 1 + residues) % node_count
    far_pick = jax.random.randint(third_key, (node_count, REMOTE * BLK_DEV), 0, BLK_DEV)
    remote_global = (peers * BLK_DEV + far_pick).reshape(node_count, BLK_DEV, REMOTE)
    joined = jnp.concatenate([local_global, remote_global], axis=2).reshape(NB, K)
    shuffles = jax.vmap(lambda single: jax.random.permutation(single, K))(jax.random.split(fourth_key, NB))
    return jnp.take_along_axis(joined, shuffles, axis=1).astype(jnp.int32)


def draw_diag_tiles(key, part):
    key = jax.random.fold_in(key, 23)
    first_key, second_key = jax.random.split(key)
    gains = jax.random.uniform(first_key, (NB, BS), jnp.float32, 0.8, 1.25)
    noise = jnp.clip(0.02 * jax.random.normal(second_key, (NB, BS, BS), jnp.float32), -0.08, 0.08)
    identity = jnp.eye(BS, dtype=jnp.float32)
    return (identity[None, :, :] * gains[:, None, :] + noise).astype(jnp.bfloat16)


def draw_precond_tiles(key, part):
    key = jax.random.fold_in(key, 37)
    first_key, second_key = jax.random.split(key)
    lambdas = jnp.exp(jax.random.uniform(first_key, (NB, BS), jnp.float32, -0.6931, 0.6931))
    raw = jnp.clip(jax.random.normal(second_key, (NB, BS, BS), jnp.float32), -2.8, 2.8)
    symmetric = 0.014 * (raw + jnp.swapaxes(raw, 1, 2))
    identity = jnp.eye(BS, dtype=jnp.float32)
    return (identity[None, :, :] * lambdas[:, None, :] + symmetric).astype(jnp.bfloat16)


def draw_right_side(key, part):
    key = jax.random.fold_in(key, 41)
    first_key = jax.random.fold_in(key, 0)
    rising = 0.35 * jnp.exp(1.0986 * jnp.arange(NB, dtype=jnp.float32) / NB)
    values = jnp.clip(jax.random.normal(first_key, (NB, NRHS, BS), jnp.float32), -4.0, 4.0)
    return values * rising[:, None, None]


def block_scale(own_key, shape, shards, smallest, high):
    def one(axis_at, parts):
        steps = jax.random.uniform(jax.random.fold_in(jax.random.fold_in(own_key, 6), axis_at), (parts,), jnp.float32, smallest / len(shards), high / len(shards))
        return jnp.repeat(jnp.exp(steps), shape[axis_at] // parts).reshape((-1,) + (1,) * (len(shape) - axis_at - 1))

    gain = one(*shards[0])
    for cut in shards[1:]:
        gain = gain * one(*cut)
    return gain


def gaussian(key, dims, width, reach, shards=(), kind=jnp.bfloat16):
    level = block_scale(key, dims, shards, -0.22, 0.18) if shards else 1.0
    values = jax.random.normal(key, dims, jnp.float32) * width * level
    return jnp.minimum(jnp.maximum(values, -reach), reach).astype(kind)


def setup_inputs(seed: int = 0) -> dict:
    keys = jax.random.split(jax.random.key(seed), 7)
    return {
        "right_side": draw_right_side(jax.random.fold_in(keys[6], 71), 0),
        "diag_tiles": draw_diag_tiles(jax.random.fold_in(keys[6], 71), 0),
        "cond_tiles": gaussian(keys[2], (NB, K, BS, BS), (16 * K * BS) ** -0.5, 0.046875, ((0, 128), (1, 2))),
        "neighbour_blocks": draw_neighbour_blocks(jax.random.fold_in(keys[6], 71), 0),
        "precision_diag": jnp.clip(jnp.exp(math.log(2.0) - 1.3862944 * jax.random.uniform(keys[4], (NB, BS), jnp.float32) ** block_scale(keys[4], (NB, BS), ((0, 128),), -0.2, 0.2)), 0.5, 2.0),
        "precond_tiles": draw_precond_tiles(jax.random.fold_in(keys[6], 71), 0),
    }


HIGH = lax.Precision.HIGHEST


def grouped(tensor):
    return tensor.reshape((NB // BLK_DEV, BLK_DEV) + tensor.shape[1:])


def apply_precision(values, diag_tiles, cond_tiles, neighbour_blocks, precision_diag):
    def forward(members):
        diag_part, cond_part, near_index, own_values, scale_part = members
        beside = values[near_index]
        summed = jnp.einsum("gts,gcs->gct", diag_part.astype(jnp.float32), own_values, precision=HIGH)
        summed = summed + jnp.einsum("gkts,gkcs->gct", cond_part.astype(jnp.float32), beside, precision=HIGH)
        return scale_part[:, None, :] * summed

    weighted = lax.map(forward, (grouped(diag_tiles), grouped(cond_tiles), grouped(neighbour_blocks),
                                 grouped(values), grouped(precision_diag)))
    weighted = weighted.reshape(values.shape)

    def diagonal_terms(members):
        diag_part, own_weighted = members
        return jnp.einsum("gts,gct->gcs", diag_part.astype(jnp.float32), own_weighted, precision=HIGH)

    own_terms = lax.map(diagonal_terms, (grouped(diag_tiles), grouped(weighted))).reshape(values.shape)

    def backward(running, members):
        cond_part, near_index, own_weighted = members
        contributions = jnp.einsum("gkts,gct->gkcs", cond_part.astype(jnp.float32), own_weighted, precision=HIGH)
        return running.at[near_index].add(contributions), None

    running, unused = lax.scan(backward, jnp.zeros(values.shape, jnp.float32),
                               (grouped(cond_tiles), grouped(neighbour_blocks), grouped(weighted)))
    return own_terms + running


def precondition(values, precond_tiles):
    return jnp.einsum("bts,bcs->bct", precond_tiles.astype(jnp.float32), values, precision=HIGH)


def reference(right_side, diag_tiles, cond_tiles, neighbour_blocks, precision_diag, precond_tiles):
    solution = jnp.zeros_like(right_side)
    residual = right_side
    shaped = precondition(residual, precond_tiles)
    direction = shaped
    gamma = jnp.sum(residual * shaped, axis=(0, 2))
    for iteration in range(ITERS):
        image = apply_precision(direction, diag_tiles, cond_tiles, neighbour_blocks, precision_diag)
        alpha = gamma / jnp.sum(direction * image, axis=(0, 2))
        solution = solution + alpha[None, :, None] * direction
        residual = residual - alpha[None, :, None] * image
        if iteration + 1 < ITERS:
            shaped = precondition(residual, precond_tiles)
            gamma_new = jnp.sum(residual * shaped, axis=(0, 2))
            direction = shaped + (gamma_new / gamma)[None, :, None] * direction
            gamma = gamma_new
    return solution, residual
```

```python
import jax
import jax.numpy as jnp
import numpy as np
from jax import lax
from jax.experimental import pallas as pl
from jax.experimental.pallas import tpu as pltpu
from jax.sharding import Mesh, PartitionSpec as P

ITERS = 3
DIMS = (8, 4, 4)
LANES = 128
COLS = 8
EXTRA = 16
LOW_EXP = -100.0
F32, BF16, I16, I32 = jnp.float32, jnp.bfloat16, jnp.int16, jnp.int32
VMEM_LIMIT = 56 * 1024 * 1024


def lane_iota():
    return lax.broadcasted_iota(I32, (COLS, LANES), 1)


def spread(column):
    return jnp.broadcast_to(column, (column.shape[0], LANES))


def split_rows(values):
    lead = values.astype(BF16).astype(F32)
    return jnp.concatenate([lead, values - lead], axis=0).astype(BF16)


def join_rows(values):
    return values[:COLS] + values[COLS:]


def encode(read, blocks, partial, write):
    lane = lane_iota()
    tops = jnp.zeros((COLS, LANES), F32)
    for block in range(blocks):
        top = jnp.max(jnp.abs(read(block)), axis=1, keepdims=True)
        tops = jnp.where(lane == block, spread(top), tops)
    total = spread(jnp.sum(partial, axis=1, keepdims=True))
    tops = jnp.where(lane == blocks, jnp.abs(total), tops)
    exps = jnp.floor(jnp.log2(jnp.maximum(tops, 1e-35))) + 1.0
    exps = jnp.clip(exps, LOW_EXP, 126.0)
    scales = jnp.exp2(15.0 - exps)
    for block in range(0, blocks, 2):
        pair = jnp.concatenate(
            [
                read(block) * spread(scales[:, block : block + 1]),
                read(block + 1) * spread(scales[:, block + 1 : block + 2]),
            ],
            axis=0,
        )
        codes = jnp.clip(jnp.round(pair), -32767.0, 32767.0)
        write(block * COLS, codes.astype(I32).astype(I16))
    scaled = total * spread(scales[:, blocks : blocks + 1]) * 0.5
    first = jnp.round(scaled)
    second = jnp.round((scaled - first) * 32768.0)
    tail = jnp.where(lane == blocks + 1, first, exps)
    tail = jnp.where(lane == blocks + 2, second, tail)
    tail = jnp.concatenate([tail, jnp.zeros_like(tail)], axis=0)
    write(blocks * COLS, tail.astype(I32).astype(I16))


def decode_tail(rows, blocks):
    tail = rows.astype(I32).astype(F32)[:COLS]
    scales = jnp.exp2(tail - 15.0)
    whole = spread(tail[:, blocks + 1 : blocks + 2])
    rest = spread(tail[:, blocks + 2 : blocks + 3])
    total = (whole + rest * (1.0 / 32768.0)) * (spread(scales[:, blocks : blocks + 1]) * 2.0)
    return scales, total


def decode_pair(rows, scales, block):
    values = rows.astype(I32).astype(F32)
    return (
        values[:COLS] * spread(scales[:, block : block + 1]),
        values[COLS:] * spread(scales[:, block + 1 : block + 2]),
    )


def start_kernel(shaped_ref, residual_ref, code_ref):
    blocks = shaped_ref.shape[0]
    partial = jnp.zeros((COLS, LANES), F32)
    for block in range(blocks):
        partial = partial + shaped_ref[block] * residual_ref[block]

    def write(row, value):
        code_ref[row : row + 2 * COLS, :] = value

    encode(lambda block: shaped_ref[block], blocks, partial, write)


def factor_kernel(first, last, peers, *refs):
    refs = list(refs)
    near_ref, me_ref, code_ref, shaped_ref, precision_ref, tiles_ref = refs[:6]
    refs = refs[6:]
    if not first:
        old_field_ref, old_direction_ref, old_gamma_ref = refs[:3]
        refs = refs[3:]
    out_ref, own_ref, direction_ref, gamma_ref = refs[:4]
    refs = refs[4:]
    field_ref, running_ref, partial_ref = refs
    step = pl.program_id(0)
    blocks = shaped_ref.shape[0]
    step_blocks = blocks // pl.num_programs(0)
    half = step_blocks // 2
    slots = 4

    @pl.when(step == 0)
    def prologue():
        gamma = jnp.zeros((COLS, LANES), F32)
        for peer in range(peers):
            gamma = gamma + decode_tail(code_ref[peer, blocks * COLS :, :], blocks)[1]
        gamma_ref[...] = gamma
        if not first:
            beta = gamma / old_gamma_ref[...]

        def take(peer, carry):
            scales, unused = decode_tail(code_ref[peer, blocks * COLS :, :], blocks)
            for block in range(0, blocks, 2):
                rows = code_ref[peer, block * COLS : (block + 2) * COLS, :]
                for offset, values in enumerate(decode_pair(rows, scales, block)):
                    place = peer * blocks + block + offset
                    if not first:
                        old = join_rows(old_field_ref[place].astype(F32))
                        values = values + beta * old
                    field_ref[place] = split_rows(values)
            return carry

        lax.fori_loop(0, peers, take, 0)
        for block in range(blocks):
            values = shaped_ref[block]
            if not first:
                values = values + beta * old_direction_ref[block]
            direction_ref[block] = values
        partial_ref[...] = jnp.zeros_like(partial_ref)

        def clear(place, carry):
            for offset in range(8):
                running_ref[place * 8 + offset] = jnp.zeros((COLS, LANES), F32)
            return carry

        lax.fori_loop(0, running_ref.shape[0] // 8, clear, 0)

    partial = partial_ref[...]
    for inner in range(step_blocks):
        block = step * step_blocks + inner
        places = [near_ref[block * 2 * slots + k] for k in range(2 * slots)]
        left = [field_ref[place] for place in places] + [split_rows(direction_ref[block])]
        right = [tiles_ref[0, core, inner * slots + slot] for core in range(2) for slot in range(slots)]
        right.append(tiles_ref[0, inner // half, slots * step_blocks + inner % half])
        left = jnp.concatenate(left, axis=1)
        right = jnp.concatenate(right, axis=1)
        summed = join_rows(
            lax.dot_general(left, right, (((1,), (1,)), ((), ())), preferred_element_type=F32)
        )
        weighted = precision_ref[pl.ds(block, 1), :] * summed
        partial = partial + weighted * summed
        pieces = join_rows(
            lax.dot_general(
                split_rows(weighted), right, (((1,), (0,)), ((), ())), preferred_element_type=F32
            )
        )
        own_ref[block] = pieces[:, 2 * slots * LANES :]
        for k, place in enumerate(places):
            running_ref[place] = running_ref[place] + pieces[:, k * LANES : (k + 1) * LANES]
    partial_ref[...] = partial

    @pl.when(step == pl.num_programs(0) - 1)
    def epilogue():
        me = me_ref[0]
        for block in range(blocks):
            own_ref[block] = own_ref[block] + running_ref[me * blocks + block]

        def give(peer, carry):
            def write(row, value):
                out_ref[peer, row : row + 2 * COLS, :] = value

            encode(lambda block: running_ref[peer * blocks + block], blocks, partial_ref[...], write)
            return carry

        lax.fori_loop(0, peers, give, 0)


def update_kernel(last, peers, *refs):
    refs = list(refs)
    me_ref, code_ref, own_ref, residual_ref, solution_ref, direction_ref, gamma_ref = refs[:7]
    refs = refs[7:]
    if last:
        new_residual_ref, new_solution_ref, image_ref = refs
    else:
        precond_ref, new_residual_ref, new_solution_ref, shaped_ref, out_ref, image_ref = refs
    blocks = own_ref.shape[0]
    me = me_ref[0]
    for block in range(blocks):
        image_ref[block] = own_ref[block]

    def take(peer, bottom):
        scales, total = decode_tail(code_ref[peer, blocks * COLS :, :], blocks)
        scales = jnp.where(peer == me, 0.0, scales)
        for block in range(0, blocks, 2):
            rows = code_ref[peer, block * COLS : (block + 2) * COLS, :]
            for offset, values in enumerate(decode_pair(rows, scales, block)):
                image_ref[block + offset] = image_ref[block + offset] + values
        return bottom + total

    bottom = lax.fori_loop(0, peers, take, jnp.zeros((COLS, LANES), F32))
    alpha = gamma_ref[...] / bottom
    partial = jnp.zeros((COLS, LANES), F32)
    for block in range(blocks):
        new_solution_ref[block] = solution_ref[block] + alpha * direction_ref[block]
        residual = residual_ref[block] - alpha * image_ref[block]
        new_residual_ref[block] = residual
        if not last:
            shaped = join_rows(
                jnp.dot(split_rows(residual), precond_ref[block], preferred_element_type=F32)
            )
            shaped_ref[block] = shaped
            partial = partial + residual * shaped
    if not last:

        def write(row, value):
            out_ref[row : row + 2 * COLS, :] = value

        encode(lambda block: shaped_ref[block], blocks, partial, write)


WHOLE = pl.BlockSpec(memory_space=pltpu.VMEM)
SCALARS = pl.BlockSpec(memory_space=pltpu.SMEM)
PARAMS = pltpu.CompilerParams(vmem_limit_bytes=VMEM_LIMIT)


def start_call(shaped, residual):
    blocks = shaped.shape[0]
    return pl.pallas_call(
        start_kernel,
        out_shape=jax.ShapeDtypeStruct((blocks * COLS + EXTRA, LANES), I16),
        in_specs=[WHOLE, WHOLE],
        out_specs=WHOLE,
        compiler_params=PARAMS,
        name="start",
    )(shaped, residual)


def factor_call(first, last, near, me, codes, shaped, precision, tiles, state):
    peers = codes.shape[0]
    blocks = shaped.shape[0]
    steps = tiles.shape[0]
    field = (peers * blocks, 2 * COLS, LANES)

    def fixed(shape):
        return pl.BlockSpec(shape, lambda step: (0,) * len(shape))

    in_specs = [SCALARS, SCALARS, fixed(codes.shape), fixed(shaped.shape), fixed(precision.shape)]
    in_specs.append(pl.BlockSpec((1,) + tiles.shape[1:], lambda step: (step, 0, 0, 0, 0)))
    in_specs += [fixed(part.shape) for part in state]
    outs = [
        (codes.shape, I16),
        (shaped.shape, F32),
        (shaped.shape, F32),
        ((COLS, LANES), F32),
    ]
    scratch = [
        pltpu.VMEM((peers * blocks, COLS, LANES), F32),
        pltpu.VMEM((COLS, LANES), F32),
    ]
    if last:
        scratch = [pltpu.VMEM(field, BF16)] + scratch
    else:
        outs.append((field, BF16))
    return pl.pallas_call(
        lambda *refs: factor_kernel(first, last, peers, *refs),
        grid=(steps,),
        out_shape=[jax.ShapeDtypeStruct(*out) for out in outs],
        in_specs=in_specs,
        out_specs=[fixed(shape) for shape, unused in outs],
        scratch_shapes=scratch,
        compiler_params=PARAMS,
        name="factor",
    )(near, me, codes, shaped, precision, tiles, *state)


def update_call(last, me, codes, own, residual, answer, direction, gamma, precond):
    shape = jax.ShapeDtypeStruct(own.shape, F32)
    outs = [shape, shape]
    arguments = [me, codes, own, residual, answer, direction, gamma]
    if not last:
        outs += [shape, jax.ShapeDtypeStruct(codes.shape[1:], I16)]
        arguments.append(precond)
    return pl.pallas_call(
        lambda *refs: update_kernel(last, codes.shape[0], *refs),
        out_shape=outs,
        in_specs=[SCALARS] + [WHOLE] * (len(arguments) - 1),
        out_specs=[WHOLE] * len(outs),
        scratch_shapes=[pltpu.VMEM(own.shape, F32)],
        compiler_params=PARAMS,
        name="update",
    )(*arguments)


def local(right_side, diag_tiles, cond_tiles, neighbour_blocks, precision_diag, precond_tiles):
    depth, wide, high = (lax.axis_size(name) for name in ("z", "x", "y"))
    peers = wide * high
    here = right_side.shape[0]
    blocks = depth * here
    core = lax.axis_index("c")
    me = (lax.axis_index("x") * high + lax.axis_index("y")).astype(I32).reshape(1)
    half = here // 2

    own_diag = lax.dynamic_slice_in_dim(diag_tiles, core * half, half, 0)
    mine = jnp.concatenate([cond_tiles.reshape(-1, LANES, LANES), own_diag], axis=0)
    tiles = lax.all_gather(mine, ("z", "c"), axis=0, tiled=False)
    tiles = tiles.reshape((depth, 2) + mine.shape)
    own_precond = lax.dynamic_slice_in_dim(precond_tiles, core * half, half, 0)
    tiles, own_precond = lax.optimization_barrier((tiles, own_precond))
    precond = lax.all_gather(own_precond, ("z", "c"), axis=0, tiled=True)

    wide_precond = precond_tiles.astype(F32)
    shaped = jnp.einsum("lts,lcs->lct", wide_precond, right_side, precision=lax.Precision.HIGHEST)
    near = jnp.pad(neighbour_blocks.astype(F32), ((0, 0), (0, LANES - neighbour_blocks.shape[1])))
    facts = jnp.concatenate([precision_diag, near], axis=0)
    facts = jnp.broadcast_to(facts[None], (depth,) + facts.shape)

    def by_column(values):
        values = values.reshape(here, depth, COLS, LANES).transpose(1, 0, 2, 3)
        return values.reshape(depth, here * COLS, LANES)

    sent = jnp.concatenate([by_column(right_side), by_column(shaped), facts], axis=1)
    came = lax.all_to_all(sent, "z", split_axis=0, concat_axis=0, tiled=True)
    rows = here * COLS
    residual = came[:, :rows].reshape(blocks, COLS, LANES)
    shaped = came[:, rows : 2 * rows].reshape(blocks, COLS, LANES)
    precision = came[:, 2 * rows : 2 * rows + here].reshape(blocks, LANES)
    near = came[:, 2 * rows + here :, : neighbour_blocks.shape[1]].astype(I32).reshape(-1)
    plane = near // (peers * here)
    near = (near // here) % peers * blocks + plane * here + near % here

    answer = jnp.zeros_like(residual)
    codes = start_call(shaped, residual)
    state = ()
    for iteration in range(ITERS):
        last = iteration + 1 == ITERS
        arrived = lax.all_gather(codes, ("x", "y"), axis=0, tiled=False)
        leaving, own, direction, gamma, *field = factor_call(
            iteration == 0, last, near, me, arrived, shaped, precision, tiles, state
        )
        terms = lax.all_to_all(leaving, ("x", "y"), split_axis=0, concat_axis=0, tiled=True)
        residual, answer, *rest = update_call(
            last, me, terms, own, residual, answer, direction, gamma, precond
        )
        if not last:
            shaped, codes = rest
            state = (field[0], direction, gamma)

    both = jnp.stack([answer, residual], axis=0).reshape(2, depth, here, COLS, LANES)
    both = lax.all_to_all(both, "z", split_axis=1, concat_axis=1, tiled=True)
    both = both.transpose(0, 2, 1, 3, 4).reshape(2, here, depth * COLS, LANES)
    return both[0], both[1]


def solution(mesh, dims=DIMS):
    grid = Mesh(np.asarray(mesh.devices).reshape(dims + (2,)), ("z", "x", "y", "c"))
    blk = ("z", "x", "y")
    return jax.shard_map(
        local,
        mesh=grid,
        in_specs=(P(blk, "c", None), P(blk), P(blk, "c"), P(blk), P(blk), P(blk)),
        out_specs=(P(blk, "c", None), P(blk, "c", None)),
        check_vma=False,
    )
```

```python
import jax
import jax.numpy as jnp
import numpy as np
from jax import lax
from jax.experimental import pallas as pl
from jax.experimental.pallas import tpu as pltpu
from jax.sharding import Mesh, PartitionSpec as P

ITERS = 3
DIMS = (8, 4, 4)
LANES = 128
COLS = 8
GROUPS = 3
EXTRA = (GROUPS + 1) * COLS
LOW_EXP = -100.0
F32, BF16, I16, I32 = jnp.float32, jnp.bfloat16, jnp.int16, jnp.int32
VMEM_LIMIT = 44 * 1024 * 1024


def spread(column):
    return jnp.broadcast_to(column, (column.shape[0], LANES))


def split_rows(values):
    lead = values.astype(BF16).astype(F32)
    return jnp.concatenate([lead, values - lead], axis=0).astype(BF16)


def join_rows(values):
    return values[:COLS] + values[COLS:]


def group_ranges(blocks):
    pairs = blocks // 2
    cuts = [2 * (pairs * part // GROUPS) for part in range(GROUPS + 1)]
    return list(zip(cuts[:-1], cuts[1:]))


def exponents(tops):
    exps = jnp.floor(jnp.log2(jnp.maximum(tops, 1e-35) * 1.0025)) + 1.0
    return jnp.clip(exps, LOW_EXP, 126.0)


def encode(read, blocks, partial, write):
    tail = []
    for low, high in group_ranges(blocks):
        tops = jnp.abs(read(low))
        for block in range(low + 1, high):
            tops = jnp.maximum(tops, jnp.abs(read(block)))
        exps = exponents(tops)
        tail.append(exps)
        scale = jnp.exp2(15.0 - exps)
        for block in range(low, high, 2):
            pair = jnp.concatenate([read(block) * scale, read(block + 1) * scale], axis=0)
            write(block * COLS, jnp.round(pair).astype(I32).astype(I16))
    total = spread(jnp.sum(partial, axis=1, keepdims=True))
    exps = exponents(jnp.abs(total))
    scaled = total * (jnp.exp2(15.0 - exps) * 0.5)
    first = jnp.round(scaled)
    second = jnp.round((scaled - first) * 32768.0)
    lane = lax.broadcasted_iota(I32, (COLS, LANES), 1)
    tail.append(jnp.where(lane == 0, exps, jnp.where(lane == 1, first, second)))
    for part in range(0, GROUPS + 1, 2):
        rows = jnp.concatenate(tail[part : part + 2], axis=0)
        write((blocks + part) * COLS, rows.astype(I32).astype(I16))


def widen(rows):
    return rows.astype(I32).astype(F32)


def decode_tail(rows):
    rows = widen(rows)
    scales = [jnp.exp2(rows[part * COLS : (part + 1) * COLS] - 15.0) for part in range(GROUPS)]
    tail = rows[GROUPS * COLS :]
    whole = tail[:, 1:2] + tail[:, 2:3] * (1.0 / 32768.0)
    total = spread(whole) * (jnp.exp2(spread(tail[:, 0:1]) - 15.0) * 2.0)
    return scales, total


def decode_blocks(read, scales, blocks, take):
    for scale, (low, high) in zip(scales, group_ranges(blocks)):
        for block in range(low, high, 2):
            values = widen(read(block * COLS))
            take(block, values[:COLS] * scale)
            take(block + 1, values[COLS:] * scale)


def start_kernel(shaped_ref, residual_ref, code_ref):
    blocks = shaped_ref.shape[0]
    partial = jnp.zeros((COLS, LANES), F32)
    for block in range(blocks):
        partial = partial + shaped_ref[block] * residual_ref[block]

    def write(row, value):
        code_ref[row : row + 2 * COLS, :] = value

    encode(lambda block: shaped_ref[block], blocks, partial, write)


def factor_kernel(first, last, peers, *refs):
    refs = list(refs)
    near_ref, me_ref, code_ref, shaped_ref, precision_ref, tiles_ref = refs[:6]
    refs = refs[6:]
    if not first:
        old_field_ref, old_direction_ref, old_gamma_ref = refs[:3]
        refs = refs[3:]
    out_ref, own_ref, direction_ref, gamma_ref = refs[:4]
    refs = refs[4:]
    field_ref, running_ref, partial_ref = refs
    step = pl.program_id(0)
    blocks = shaped_ref.shape[0]
    step_blocks = blocks // pl.num_programs(0)
    half = step_blocks // 2
    slots = 4

    @pl.when(step == 0)
    def prologue():
        gamma = jnp.zeros((COLS, LANES), F32)
        for peer in range(peers):
            gamma = gamma + decode_tail(code_ref[peer, blocks * COLS :, :])[1]
        gamma_ref[...] = gamma
        if not first:
            beta = gamma / old_gamma_ref[...]

        def take(peer, carry):
            scales, unused = decode_tail(code_ref[peer, blocks * COLS :, :])

            def keep(block, values):
                place = peer * blocks + block
                if not first:
                    values = values + beta * join_rows(old_field_ref[place].astype(F32))
                field_ref[place] = split_rows(values)

            def read(row):
                return code_ref[peer, row : row + 2 * COLS, :]

            decode_blocks(read, scales, blocks, keep)
            return carry

        lax.fori_loop(0, peers, take, 0)
        for block in range(blocks):
            values = shaped_ref[block]
            if not first:
                values = values + beta * old_direction_ref[block]
            direction_ref[block] = values
        partial_ref[...] = jnp.zeros_like(partial_ref)

        def clear(place, carry):
            for offset in range(8):
                running_ref[place * 8 + offset] = jnp.zeros((COLS, LANES), F32)
            return carry

        lax.fori_loop(0, running_ref.shape[0] // 8, clear, 0)

    def tile_row(inner):
        parts = [tiles_ref[0, core, inner * slots + slot] for core in range(2) for slot in range(slots)]
        parts.append(tiles_ref[0, inner // half, slots * step_blocks + inner % half])
        return jnp.concatenate(parts, axis=1)

    partial = partial_ref[...]
    kept = []
    for inner in range(step_blocks):
        block = step * step_blocks + inner
        places = [near_ref[block * 2 * slots + k] for k in range(2 * slots)]
        left = [field_ref[place] for place in places] + [split_rows(direction_ref[block])]
        summed = join_rows(
            lax.dot_general(
                jnp.concatenate(left, axis=1),
                tile_row(inner),
                (((1,), (1,)), ((), ())),
                preferred_element_type=F32,
            )
        )
        weighted = precision_ref[pl.ds(block, 1), :] * summed
        partial = partial + weighted * summed
        kept.append((block, places, split_rows(weighted)))
    for inner, (block, places, weighted) in enumerate(kept):
        pieces = join_rows(
            jnp.dot(weighted, tile_row(inner), preferred_element_type=F32)
        )
        own_ref[block] = pieces[:, 2 * slots * LANES :]
        for k, place in enumerate(places):
            running_ref[place] = running_ref[place] + pieces[:, k * LANES : (k + 1) * LANES]
    partial_ref[...] = partial

    @pl.when(step == pl.num_programs(0) - 1)
    def epilogue():
        me = me_ref[0]
        for block in range(blocks):
            own_ref[block] = own_ref[block] + running_ref[me * blocks + block]

        def give(peer, carry):
            def write(row, value):
                out_ref[peer, row : row + 2 * COLS, :] = value

            encode(lambda block: running_ref[peer * blocks + block], blocks, partial_ref[...], write)
            return carry

        lax.fori_loop(0, peers, give, 0)


def update_kernel(last, peers, *refs):
    refs = list(refs)
    me_ref, code_ref, own_ref, residual_ref, solution_ref, direction_ref, gamma_ref = refs[:7]
    refs = refs[7:]
    if last:
        new_residual_ref, new_solution_ref, image_ref = refs
    else:
        precond_ref, new_residual_ref, new_solution_ref, shaped_ref, out_ref, image_ref = refs
    blocks = own_ref.shape[0]
    me = me_ref[0]
    for block in range(blocks):
        image_ref[block] = own_ref[block]

    def take(peer, bottom):
        scales, total = decode_tail(code_ref[peer, blocks * COLS :, :])
        scales = [jnp.where(peer == me, 0.0, scale) for scale in scales]

        def read(row):
            return code_ref[peer, row : row + 2 * COLS, :]

        def add(block, values):
            image_ref[block] = image_ref[block] + values

        decode_blocks(read, scales, blocks, add)
        return bottom + total

    bottom = lax.fori_loop(0, peers, take, jnp.zeros((COLS, LANES), F32))
    alpha = gamma_ref[...] / bottom
    partial = jnp.zeros((COLS, LANES), F32)
    for block in range(blocks):
        new_solution_ref[block] = solution_ref[block] + alpha * direction_ref[block]
        residual = residual_ref[block] - alpha * image_ref[block]
        new_residual_ref[block] = residual
        if not last:
            shaped = join_rows(
                jnp.dot(split_rows(residual), precond_ref[block], preferred_element_type=F32)
            )
            shaped_ref[block] = shaped
            partial = partial + residual * shaped
    if not last:

        def write(row, value):
            out_ref[row : row + 2 * COLS, :] = value

        encode(lambda block: shaped_ref[block], blocks, partial, write)


WHOLE = pl.BlockSpec(memory_space=pltpu.VMEM)
SCALARS = pl.BlockSpec(memory_space=pltpu.SMEM)
PARAMS = pltpu.CompilerParams(vmem_limit_bytes=VMEM_LIMIT)


def start_call(shaped, residual):
    blocks = shaped.shape[0]
    return pl.pallas_call(
        start_kernel,
        out_shape=jax.ShapeDtypeStruct((blocks * COLS + EXTRA, LANES), I16),
        in_specs=[WHOLE, WHOLE],
        out_specs=WHOLE,
        compiler_params=PARAMS,
        name="start",
    )(shaped, residual)


def factor_call(first, last, near, me, codes, shaped, precision, tiles, state):
    peers = codes.shape[0]
    blocks = shaped.shape[0]
    steps = tiles.shape[0]
    field = (peers * blocks, 2 * COLS, LANES)

    in_specs = [SCALARS, SCALARS, WHOLE, WHOLE, WHOLE]
    in_specs.append(pl.BlockSpec((1,) + tiles.shape[1:], lambda step: (step, 0, 0, 0, 0)))
    in_specs += [WHOLE] * len(state)
    outs = [
        (codes.shape, I16),
        (shaped.shape, F32),
        (shaped.shape, F32),
        ((COLS, LANES), F32),
    ]
    scratch = [
        pltpu.VMEM((peers * blocks, COLS, LANES), F32),
        pltpu.VMEM((COLS, LANES), F32),
    ]
    if last:
        scratch = [pltpu.VMEM(field, BF16)] + scratch
    else:
        outs.append((field, BF16))
    return pl.pallas_call(
        lambda *refs: factor_kernel(first, last, peers, *refs),
        grid=(steps,),
        out_shape=[jax.ShapeDtypeStruct(*out) for out in outs],
        in_specs=in_specs,
        out_specs=[WHOLE] * len(outs),
        scratch_shapes=scratch,
        compiler_params=PARAMS,
        name="factor",
    )(near, me, codes, shaped, precision, tiles, *state)


def update_call(last, me, codes, own, residual, answer, direction, gamma, precond):
    shape = jax.ShapeDtypeStruct(own.shape, F32)
    outs = [shape, shape]
    arguments = [me, codes, own, residual, answer, direction, gamma]
    if not last:
        outs += [shape, jax.ShapeDtypeStruct(codes.shape[1:], I16)]
        arguments.append(precond)
    return pl.pallas_call(
        lambda *refs: update_kernel(last, codes.shape[0], *refs),
        out_shape=outs,
        in_specs=[SCALARS] + [WHOLE] * (len(arguments) - 1),
        out_specs=[WHOLE] * len(outs),
        scratch_shapes=[pltpu.VMEM(own.shape, F32)],
        compiler_params=PARAMS,
        name="update",
    )(*arguments)


def local(right_side, diag_tiles, cond_tiles, neighbour_blocks, precision_diag, precond_tiles):
    depth, wide, high = (lax.axis_size(name) for name in ("z", "x", "y"))
    peers = wide * high
    here = right_side.shape[0]
    blocks = depth * here
    core = lax.axis_index("c")
    me = (lax.axis_index("x") * high + lax.axis_index("y")).astype(I32).reshape(1)
    half = here // 2

    own_diag = lax.dynamic_slice_in_dim(diag_tiles, core * half, half, 0)
    mine = jnp.concatenate([cond_tiles.reshape(-1, LANES, LANES), own_diag], axis=0)
    tiles = lax.all_gather(mine, ("z", "c"), axis=0, tiled=False)
    tiles = tiles.reshape((depth, 2) + mine.shape)
    own_precond = lax.dynamic_slice_in_dim(precond_tiles, core * half, half, 0)

    wide_precond = precond_tiles.astype(F32)
    shaped = jnp.einsum("lts,lcs->lct", wide_precond, right_side, precision=lax.Precision.HIGHEST)
    near = jnp.pad(neighbour_blocks.astype(F32), ((0, 0), (0, LANES - neighbour_blocks.shape[1])))
    facts = jnp.concatenate([precision_diag, near], axis=0)
    facts = jnp.broadcast_to(facts[None], (depth,) + facts.shape)

    def by_column(values):
        values = values.reshape(here, depth, COLS, LANES).transpose(1, 0, 2, 3)
        return values.reshape(depth, here * COLS, LANES)

    sent = jnp.concatenate([by_column(right_side), by_column(shaped), facts], axis=1)
    came = lax.all_to_all(sent, "z", split_axis=0, concat_axis=0, tiled=True)
    rows = here * COLS
    residual = came[:, :rows].reshape(blocks, COLS, LANES)
    shaped = came[:, rows : 2 * rows].reshape(blocks, COLS, LANES)
    precision = came[:, 2 * rows : 2 * rows + here].reshape(blocks, LANES)
    near = came[:, 2 * rows + here :, : neighbour_blocks.shape[1]].astype(I32).reshape(-1)
    plane = near // (peers * here)
    near = (near // here) % peers * blocks + plane * here + near % here

    answer = jnp.zeros_like(residual)
    codes = start_call(shaped, residual)
    state = ()
    for iteration in range(ITERS):
        last = iteration + 1 == ITERS
        arrived = lax.all_gather(codes, ("x", "y"), axis=0, tiled=False)
        if iteration == 0:
            arrived, tiles, own_precond = lax.optimization_barrier((arrived, tiles, own_precond))
            precond = lax.all_gather(own_precond, ("z", "c"), axis=0, tiled=True)
        leaving, own, direction, gamma, *field = factor_call(
            iteration == 0, last, near, me, arrived, shaped, precision, tiles, state
        )
        terms = lax.all_to_all(leaving, ("x", "y"), split_axis=0, concat_axis=0, tiled=True)
        residual, answer, *rest = update_call(
            last, me, terms, own, residual, answer, direction, gamma, precond
        )
        if not last:
            shaped, codes = rest
            state = (field[0], direction, gamma)

    both = jnp.stack([answer, residual], axis=0).reshape(2, depth, here, COLS, LANES)
    both = lax.all_to_all(both, "z", split_axis=1, concat_axis=1, tiled=True)
    both = both.transpose(0, 2, 1, 3, 4).reshape(2, here, depth * COLS, LANES)
    return both[0], both[1]


def solution(mesh, dims=DIMS):
    grid = Mesh(np.asarray(mesh.devices).reshape(dims + (2,)), ("z", "x", "y", "c"))
    blk = ("z", "x", "y")
    return jax.shard_map(
        local,
        mesh=grid,
        in_specs=(P(blk, "c", None), P(blk), P(blk, "c"), P(blk), P(blk), P(blk)),
        out_specs=(P(blk, "c", None), P(blk, "c", None)),
        check_vma=False,
    )
```

```python
import jax
import jax.numpy as jnp
import numpy as np
from jax import lax
from jax.experimental import pallas as pl
from jax.experimental.pallas import tpu as pltpu
from jax.sharding import Mesh, PartitionSpec as P

ITERS = 3
DIMS = (8, 4, 4)
LANES = 128
COLS = 8
SHARE = 8
SLOTS = 4
GROUPS = 3
EXTRA = (GROUPS + 1) * COLS
LOW_EXP = -100.0
F32, BF16, I16, I32 = jnp.float32, jnp.bfloat16, jnp.int16, jnp.int32
VMEM_LIMIT = 12 * 1024 * 1024


def spread(column):
    return jnp.broadcast_to(column, (column.shape[0], LANES))


def split_rows(values):
    lead = values.astype(BF16).astype(F32)
    return jnp.concatenate([lead, values - lead], axis=0).astype(BF16)


def join_rows(values):
    return values[:COLS] + values[COLS:]


def group_ranges(blocks):
    pairs = blocks // 2
    cuts = [2 * (pairs * part // GROUPS) for part in range(GROUPS + 1)]
    return list(zip(cuts[:-1], cuts[1:]))


def exponents(tops):
    exps = jnp.floor(jnp.log2(jnp.maximum(tops, 1e-35) * 1.0025)) + 1.0
    return jnp.clip(exps, LOW_EXP, 126.0)


def encode(read, blocks, partial, write):
    tail = []
    for low, high in group_ranges(blocks):
        tops = jnp.abs(read(low))
        for block in range(low + 1, high):
            tops = jnp.maximum(tops, jnp.abs(read(block)))
        exps = exponents(tops)
        tail.append(exps)
        scale = jnp.exp2(15.0 - exps)
        for block in range(low, high, 2):
            pair = jnp.concatenate([read(block) * scale, read(block + 1) * scale], axis=0)
            write(block * COLS, jnp.round(pair).astype(I32).astype(I16))
    total = spread(jnp.sum(partial, axis=1, keepdims=True))
    exps = exponents(jnp.abs(total))
    scaled = total * (jnp.exp2(15.0 - exps) * 0.5)
    first = jnp.round(scaled)
    second = jnp.round((scaled - first) * 32768.0)
    lane = lax.broadcasted_iota(I32, (COLS, LANES), 1)
    tail.append(jnp.where(lane == 0, exps, jnp.where(lane == 1, first, second)))
    for part in range(0, GROUPS + 1, 2):
        rows = jnp.concatenate(tail[part : part + 2], axis=0)
        write((blocks + part) * COLS, rows.astype(I32).astype(I16))


def widen(rows):
    return rows.astype(I32).astype(F32)


def decode_tail(rows):
    rows = widen(rows)
    scales = [jnp.exp2(rows[part * COLS : (part + 1) * COLS] - 15.0) for part in range(GROUPS)]
    tail = rows[GROUPS * COLS :]
    whole = tail[:, 1:2] + tail[:, 2:3] * (1.0 / 32768.0)
    total = spread(whole) * (jnp.exp2(spread(tail[:, 0:1]) - 15.0) * 2.0)
    return scales, total


def decode_blocks(read, scales, blocks, take):
    for scale, (low, high) in zip(scales, group_ranges(blocks)):
        for block in range(low, high, 2):
            values = widen(read(block * COLS))
            take(block, values[:COLS] * scale)
            take(block + 1, values[COLS:] * scale)


def start_kernel(shaped_ref, residual_ref, code_ref):
    blocks = shaped_ref.shape[0]
    partial = jnp.zeros((COLS, LANES), F32)
    for block in range(blocks):
        partial = partial + shaped_ref[block] * residual_ref[block]

    def write(row, value):
        code_ref[row : row + 2 * COLS, :] = value

    encode(lambda block: shaped_ref[block], blocks, partial, write)


def total_gamma(code_ref, blocks):
    gamma = jnp.zeros((COLS, LANES), F32)
    for peer in range(code_ref.shape[0]):
        gamma = gamma + decode_tail(code_ref[peer, blocks * COLS :, :])[1]
    return gamma


def fill_field(code_ref, blocks, correct, field_ref, running_ref):
    def take(peer, carry):
        scales, unused = decode_tail(code_ref[peer, blocks * COLS :, :])

        def keep(block, values):
            place = peer * blocks + block
            field_ref[place] = split_rows(correct(place, values))
            running_ref[place] = jnp.zeros((COLS, LANES), F32)

        def read(row):
            return code_ref[peer, row : row + 2 * COLS, :]

        decode_blocks(read, scales, blocks, keep)
        return carry

    lax.fori_loop(0, code_ref.shape[0], take, 0)


def products(tile, core, plane, near_ref, direction_ref, precision_ref, field_ref, sums):
    own_ref, running_ref, partial_ref = sums
    half = SHARE // 2
    partial = partial_ref[...]
    kept = []
    for inner in range(SHARE):
        side = inner // half
        local_block = lax.rem(core + side, 2) * half + inner % half
        block = plane * SHARE + local_block
        places = []
        for part in range(2):
            first = block * 2 * SLOTS + lax.rem(core + part, 2) * SLOTS
            places += [near_ref[first + slot] for slot in range(SLOTS)]

        def tile_row(local_block=local_block, side=side, inner=inner):
            parts = [
                tile(part, local_block * SLOTS + slot) for part in range(2) for slot in range(SLOTS)
            ]
            parts.append(tile(side, SLOTS * SHARE + inner % half))
            return jnp.concatenate(parts, axis=1)

        left = [field_ref[place] for place in places] + [split_rows(direction_ref[block])]
        summed = join_rows(
            lax.dot_general(
                jnp.concatenate(left, axis=1),
                tile_row(),
                (((1,), (1,)), ((), ())),
                preferred_element_type=F32,
            )
        )
        weighted = precision_ref[pl.ds(block, 1), :] * summed
        partial = partial + weighted * summed
        kept.append((block, places, split_rows(weighted), tile_row))
    partial_ref[...] = partial
    for block, places, weighted, tile_row in kept:
        pieces = join_rows(jnp.dot(weighted, tile_row(), preferred_element_type=F32))
        own_ref[block] = pieces[:, 2 * SLOTS * LANES :]
        for k, place in enumerate(places):
            running_ref[place] = running_ref[place] + pieces[:, k * LANES : (k + 1) * LANES]


def give_codes(me, blocks, own_ref, running_ref, partial_ref, out_ref):
    for block in range(blocks):
        own_ref[block] = own_ref[block] + running_ref[me * blocks + block]

    def give(peer, carry):
        def write(row, value):
            out_ref[peer, row : row + 2 * COLS, :] = value

        encode(lambda block: running_ref[peer * blocks + block], blocks, partial_ref[...], write)
        return carry

    lax.fori_loop(0, out_ref.shape[0], give, 0)


def stage_kernel(first, last, planes, *refs):
    refs = list(refs)
    near_ref, ints_ref, shaped_ref, precision_ref = refs[:4]
    tile_refs = refs[4 : 4 + 2 * planes]
    refs = refs[4 + 2 * planes :]
    blocks = shaped_ref.shape[0]
    if first:
        code_ref, kept_ref, own_ref, running_ref, partial_ref, field_ref, gamma_ref = refs
        gamma_ref[...] = total_gamma(code_ref, blocks)
        fill_field(code_ref, blocks, lambda place, values: values, field_ref, running_ref)
        partial_ref[...] = jnp.zeros_like(partial_ref)
        own_ref[...] = jnp.zeros_like(own_ref)
    else:
        field_ref, old_own_ref, old_running_ref, old_partial_ref = refs[:4]
        kept_ref, own_ref, running_ref, partial_ref = refs[4:8]
        partial_ref[...] = old_partial_ref[...]
        own_ref[...] = old_own_ref[...]

        def carry_over(place, carry):
            for step in range(8):
                running_ref[place * 8 + step] = old_running_ref[place * 8 + step]
            return carry

        lax.fori_loop(0, running_ref.shape[0] // 8, carry_over, 0)

    def keep(index, carry):
        for plane in range(planes):
            for part in range(2):
                kept_ref[plane, part, index] = tile_refs[2 * plane + part][index]
        return carry

    lax.fori_loop(0, kept_ref.shape[2], keep, 0)

    def work(plane, carry):
        products(
            lambda part, index: kept_ref[plane, part, index],
            ints_ref[1],
            ints_ref[2 + plane],
            near_ref,
            shaped_ref,
            precision_ref,
            field_ref,
            (own_ref, running_ref, partial_ref),
        )
        return carry

    lax.fori_loop(0, planes, work, 0)
    if last:
        give_codes(ints_ref[0], blocks, own_ref, running_ref, partial_ref, refs[8])


def factor_kernel(last, groups, *refs):
    refs = list(refs)
    near_ref, ints_ref, code_ref, shaped_ref, precision_ref = refs[:5]
    old_field_ref, old_direction_ref, old_gamma_ref = refs[5:8]
    tile_refs = refs[8 : 8 + groups]
    out_ref, own_ref, direction_ref, gamma_ref, field_ref, running_ref, partial_ref = refs[8 + groups :]
    blocks = shaped_ref.shape[0]
    gamma = total_gamma(code_ref, blocks)
    gamma_ref[...] = gamma
    beta = gamma / old_gamma_ref[...]

    def correct(place, values):
        return values + beta * join_rows(old_field_ref[place].astype(F32))

    fill_field(code_ref, blocks, correct, field_ref, running_ref)
    for block in range(blocks):
        direction_ref[block] = shaped_ref[block] + beta * old_direction_ref[block]
    partial_ref[...] = jnp.zeros_like(partial_ref)
    offset = 2
    for tile_ref in tile_refs:
        planes = tile_ref.shape[0]

        def work(plane, carry, tile_ref=tile_ref, offset=offset):
            products(
                lambda part, index: tile_ref[plane, part, index],
                ints_ref[1],
                ints_ref[offset + plane],
                near_ref,
                direction_ref,
                precision_ref,
                field_ref,
                (own_ref, running_ref, partial_ref),
            )
            return carry

        lax.fori_loop(0, planes, work, 0)
        offset += planes
    give_codes(ints_ref[0], blocks, own_ref, running_ref, partial_ref, out_ref)


def update_kernel(last, peers, *refs):
    refs = list(refs)
    me_ref, code_ref, own_ref, residual_ref, solution_ref, direction_ref, gamma_ref = refs[:7]
    refs = refs[7:]
    if last:
        new_residual_ref, new_solution_ref, image_ref = refs
    else:
        precond_ref, new_residual_ref, new_solution_ref, shaped_ref, out_ref, image_ref = refs
    blocks = own_ref.shape[0]
    me = me_ref[0]
    for block in range(blocks):
        image_ref[block] = own_ref[block]

    def take(peer, bottom):
        scales, total = decode_tail(code_ref[peer, blocks * COLS :, :])
        scales = [jnp.where(peer == me, 0.0, scale) for scale in scales]

        def read(row):
            return code_ref[peer, row : row + 2 * COLS, :]

        def add(block, values):
            image_ref[block] = image_ref[block] + values

        decode_blocks(read, scales, blocks, add)
        return bottom + total

    bottom = lax.fori_loop(0, peers, take, jnp.zeros((COLS, LANES), F32))
    alpha = gamma_ref[...] / bottom
    partial = jnp.zeros((COLS, LANES), F32)
    for block in range(blocks):
        new_solution_ref[block] = solution_ref[block] + alpha * direction_ref[block]
        residual = residual_ref[block] - alpha * image_ref[block]
        new_residual_ref[block] = residual
        if not last:
            shaped = join_rows(
                jnp.dot(split_rows(residual), precond_ref[block], preferred_element_type=F32)
            )
            shaped_ref[block] = shaped
            partial = partial + residual * shaped
    if not last:

        def write(row, value):
            out_ref[row : row + 2 * COLS, :] = value

        encode(lambda block: shaped_ref[block], blocks, partial, write)


WHOLE = pl.BlockSpec(memory_space=pltpu.VMEM)
SCALARS = pl.BlockSpec(memory_space=pltpu.SMEM)
PARAMS = pltpu.CompilerParams(vmem_limit_bytes=VMEM_LIMIT)


def start_call(shaped, residual):
    blocks = shaped.shape[0]
    return pl.pallas_call(
        start_kernel,
        out_shape=jax.ShapeDtypeStruct((blocks * COLS + EXTRA, LANES), I16),
        in_specs=[WHOLE, WHOLE],
        out_specs=WHOLE,
        compiler_params=PARAMS,
        name="start",
    )(shaped, residual)


def stage_call(first, last, near, ints, shaped, precision, tiles, state):
    planes = len(tiles) // 2
    if first:
        peers = state[0].shape[0]
    else:
        peers = state[0].shape[0] // shaped.shape[0]
    blocks = shaped.shape[0]
    places = peers * blocks
    outs = [
        ((planes, 2) + tiles[0].shape, BF16),
        (shaped.shape, F32),
        ((places, COLS, LANES), F32),
        ((COLS, LANES), F32),
    ]
    if first:
        outs += [((places, 2 * COLS, LANES), BF16), ((COLS, LANES), F32)]
    if last:
        outs.append(((peers, blocks * COLS + EXTRA, LANES), I16))
    arguments = (near, ints, shaped, precision, *tiles, *state)
    tile_count = planes * SHARE * (2 * SLOTS + 1)
    return pl.pallas_call(
        lambda *refs: stage_kernel(first, last, planes, *refs),
        out_shape=[jax.ShapeDtypeStruct(*out) for out in outs],
        in_specs=[SCALARS, SCALARS] + [WHOLE] * (len(arguments) - 2),
        out_specs=[WHOLE] * len(outs),
        compiler_params=PARAMS,
        cost_estimate=pl.CostEstimate(
            flops=tile_count * 4 * LANES * LANES * LANES, bytes_accessed=10_000_000, transcendentals=0
        ),
        name="stage",
    )(*arguments)


def factor_call(last, near, ints, codes, shaped, precision, state, tiles):
    peers = codes.shape[0]
    blocks = shaped.shape[0]
    field = (peers * blocks, 2 * COLS, LANES)
    arguments = (near, ints, codes, shaped, precision, *state, *tiles)
    outs = [
        (codes.shape, I16),
        (shaped.shape, F32),
        (shaped.shape, F32),
        ((COLS, LANES), F32),
    ]
    scratch = [
        pltpu.VMEM((peers * blocks, COLS, LANES), F32),
        pltpu.VMEM((COLS, LANES), F32),
    ]
    if last:
        scratch = [pltpu.VMEM(field, BF16)] + scratch
    else:
        outs.append((field, BF16))
    return pl.pallas_call(
        lambda *refs: factor_kernel(last, len(tiles), *refs),
        out_shape=[jax.ShapeDtypeStruct(*out) for out in outs],
        in_specs=[SCALARS, SCALARS] + [WHOLE] * (len(arguments) - 2),
        out_specs=[WHOLE] * len(outs),
        scratch_shapes=scratch,
        compiler_params=PARAMS,
        name="factor",
    )(*arguments)


def update_call(last, me, codes, own, residual, answer, direction, gamma, precond):
    shape = jax.ShapeDtypeStruct(own.shape, F32)
    outs = [shape, shape]
    arguments = [me, codes, own, residual, answer, direction, gamma]
    if not last:
        outs += [shape, jax.ShapeDtypeStruct(codes.shape[1:], I16)]
        arguments.append(precond)
    return pl.pallas_call(
        lambda *refs: update_kernel(last, codes.shape[0], *refs),
        out_shape=outs,
        in_specs=[SCALARS] + [WHOLE] * (len(arguments) - 1),
        out_specs=[WHOLE] * len(outs),
        scratch_shapes=[pltpu.VMEM(own.shape, F32)],
        compiler_params=PARAMS,
        name="update",
    )(*arguments)


def shift(values, name, by):
    size = lax.axis_size(name)
    return lax.ppermute(values, name, [(index, (index + by) % size) for index in range(size)])


def local(right_side, diag_tiles, cond_tiles, neighbour_blocks, precision_diag, precond_tiles):
    depth, wide, high = (lax.axis_size(name) for name in ("z", "x", "y"))
    peers = wide * high
    here = right_side.shape[0]
    blocks = depth * here
    core = lax.axis_index("c")
    me = (lax.axis_index("x") * high + lax.axis_index("y")).astype(I32).reshape(1)
    half = here // 2

    own_diag = lax.dynamic_slice_in_dim(diag_tiles, core * half, half, 0)
    mine = jnp.concatenate([cond_tiles.reshape(-1, LANES, LANES), own_diag], axis=0)
    own_precond = lax.dynamic_slice_in_dim(precond_tiles, core * half, half, 0)

    place = lax.axis_index("z")
    other = shift(mine, "c", 1)
    steps = (depth - 1) // 2
    cut = mine.shape[0] // 2
    ups, downs = [mine], [mine]

    wide_precond = precond_tiles.astype(F32)
    shaped = jnp.einsum("lts,lcs->lct", wide_precond, right_side, precision=lax.Precision.HIGHEST)
    near = jnp.pad(neighbour_blocks.astype(F32), ((0, 0), (0, LANES - neighbour_blocks.shape[1])))
    facts = jnp.concatenate([precision_diag, near], axis=0)
    facts = jnp.broadcast_to(facts[None], (depth,) + facts.shape)

    def by_column(values):
        values = values.reshape(here, depth, COLS, LANES).transpose(1, 0, 2, 3)
        return values.reshape(depth, here * COLS, LANES)

    sent = jnp.concatenate([by_column(right_side), by_column(shaped), facts], axis=1)
    came = lax.all_to_all(sent, "z", split_axis=0, concat_axis=0, tiled=True)
    rows = here * COLS
    residual = came[:, :rows].reshape(blocks, COLS, LANES)
    shaped = came[:, rows : 2 * rows].reshape(blocks, COLS, LANES)
    precision = came[:, 2 * rows : 2 * rows + here].reshape(blocks, LANES)
    near = came[:, 2 * rows + here :, : neighbour_blocks.shape[1]].astype(I32).reshape(-1)
    plane = near // (peers * here)
    near = (near // here) % peers * blocks + plane * here + near % here

    answer = jnp.zeros_like(residual)
    codes = start_call(shaped, residual)
    if steps:
        ups.append(shift(mine, "z", 1))
        downs.append(shift(mine, "z", -1))
        codes, ups[1], downs[1], own_precond = lax.optimization_barrier(
            (codes, ups[1], downs[1], own_precond)
        )
    precond = lax.all_gather(own_precond, ("z", "c"), axis=0, tiled=True)
    arrived = lax.all_gather(codes, ("x", "y"), axis=0, tiled=False)

    def both_cores(values):
        return [values, shift(values, "c", 1)]

    def planes(step):
        return [(place - step) % depth, (place + step) % depth]

    tiles = []

    def stage(first, last, parts, which, state):
        ints = jnp.stack([me[0], core.astype(I32)] + which).astype(I32)
        kept, own, running, partial, *rest = stage_call(
            first, last, near, ints, shaped, precision, parts, state
        )
        tiles.append(kept)
        return own, running, partial, rest

    parts, which = [mine, other], [place]
    if steps:
        parts += both_cores(ups[1]) + both_cores(downs[1])
        which += planes(1)
    if steps > 1:
        ups.append(shift(ups[1], "z", 1))
        downs.append(shift(downs[1], "z", -1))
        arrived, ups[2], downs[2] = lax.optimization_barrier((arrived, ups[2], downs[2]))
    own, running, partial, (field, gamma) = stage(True, False, parts, which, (arrived,))
    for step in range(2, steps + 1):
        parts = both_cores(ups[step]) + both_cores(downs[step])
        if step < steps:
            ups.append(shift(ups[step], "z", 1))
            downs.append(shift(downs[step], "z", -1))
            partial, ups[step + 1], downs[step + 1] = lax.optimization_barrier(
                (partial, ups[step + 1], downs[step + 1])
            )
        else:
            middle = [shift(ups[step][:cut], "z", 1), shift(downs[step][cut:], "z", -1)]
            partial, precond, *middle = lax.optimization_barrier((partial, precond, *middle))
        own, running, partial, unused = stage(
            False, False, parts, planes(step), (field, own, running, partial)
        )
    if steps < 2:
        middle = [shift(ups[-1][:cut], "z", 1), shift(downs[-1][cut:], "z", -1)]
    across = [shift(values, "c", 1) for values in middle]
    parts = [jnp.concatenate(middle, axis=0), jnp.concatenate(across, axis=0)]
    own, running, partial, rest = stage(
        False, True, parts, planes(depth // 2)[:1], (field, own, running, partial)
    )
    leaving = rest[-1]
    direction = shaped
    order = [place]
    for step in range(1, steps + 1):
        order += planes(step)
    order.append(planes(depth // 2)[0])
    for iteration in range(ITERS):
        last = iteration + 1 == ITERS
        if iteration:
            arrived = lax.all_gather(codes, ("x", "y"), axis=0, tiled=False)
            ints = jnp.stack([me[0], core.astype(I32)] + order).astype(I32)
            leaving, own, direction, gamma, *rest = factor_call(
                last, near, ints, arrived, shaped, precision, (field, direction, gamma), tiles
            )
            if not last:
                field = rest[0]
        terms = lax.all_to_all(leaving, ("x", "y"), split_axis=0, concat_axis=0, tiled=True)
        residual, answer, *rest = update_call(
            last, me, terms, own, residual, answer, direction, gamma, precond
        )
        if not last:
            shaped, codes = rest

    both = jnp.stack([answer, residual], axis=0).reshape(2, depth, here, COLS, LANES)
    both = lax.all_to_all(both, "z", split_axis=1, concat_axis=1, tiled=True)
    both = both.transpose(0, 2, 1, 3, 4).reshape(2, here, depth * COLS, LANES)
    return both[0], both[1]


def solution(mesh, dims=DIMS):
    grid = Mesh(np.asarray(mesh.devices).reshape(dims + (2,)), ("z", "x", "y", "c"))
    blk = ("z", "x", "y")
    return jax.shard_map(
        local,
        mesh=grid,
        in_specs=(P(blk, "c", None), P(blk), P(blk, "c"), P(blk), P(blk), P(blk)),
        out_specs=(P(blk, "c", None), P(blk, "c", None)),
        check_vma=False,
    )
```

```python
import jax
import jax.numpy as jnp
import numpy as np
from jax import lax
from jax.experimental import pallas as pl
from jax.experimental.pallas import tpu as pltpu
from jax.sharding import Mesh, PartitionSpec as P

ITERS = 3
DIMS = (8, 4, 4)
LANES = 128
COLS = 8
GROUPS = 3
EXTRA = (GROUPS + 1) * COLS
BUFFERS = 4
LOW_EXP = -100.0
F32, BF16, I16, I32 = jnp.float32, jnp.bfloat16, jnp.int16, jnp.int32
VMEM_LIMIT = 46 * 1024 * 1024


def spread(column):
    return jnp.broadcast_to(column, (column.shape[0], LANES))


def split_rows(values):
    lead = values.astype(BF16).astype(F32)
    return jnp.concatenate([lead, values - lead], axis=0).astype(BF16)


def join_rows(values):
    return values[:COLS] + values[COLS:]


def group_ranges(blocks):
    pairs = blocks // 2
    cuts = [2 * (pairs * part // GROUPS) for part in range(GROUPS + 1)]
    return list(zip(cuts[:-1], cuts[1:]))


def exponents(tops):
    exps = jnp.floor(jnp.log2(jnp.maximum(tops, 1e-35) * 1.0025)) + 1.0
    return jnp.clip(exps, LOW_EXP, 126.0)


def encode(read, blocks, partial, write):
    tail = []
    for low, high in group_ranges(blocks):
        tops = jnp.abs(read(low))
        for block in range(low + 1, high):
            tops = jnp.maximum(tops, jnp.abs(read(block)))
        exps = exponents(tops)
        tail.append(exps)
        scale = jnp.exp2(15.0 - exps)
        for block in range(low, high, 2):
            pair = jnp.concatenate([read(block) * scale, read(block + 1) * scale], axis=0)
            write(block * COLS, jnp.round(pair).astype(I32).astype(I16))
    total = spread(jnp.sum(partial, axis=1, keepdims=True))
    exps = exponents(jnp.abs(total))
    scaled = total * (jnp.exp2(15.0 - exps) * 0.5)
    first = jnp.round(scaled)
    second = jnp.round((scaled - first) * 32768.0)
    lane = lax.broadcasted_iota(I32, (COLS, LANES), 1)
    tail.append(jnp.where(lane == 0, exps, jnp.where(lane == 1, first, second)))
    for part in range(0, GROUPS + 1, 2):
        rows = jnp.concatenate(tail[part : part + 2], axis=0)
        write((blocks + part) * COLS, rows.astype(I32).astype(I16))


def widen(rows):
    return rows.astype(I32).astype(F32)


def decode_tail(rows):
    rows = widen(rows)
    scales = [jnp.exp2(rows[part * COLS : (part + 1) * COLS] - 15.0) for part in range(GROUPS)]
    tail = rows[GROUPS * COLS :]
    whole = tail[:, 1:2] + tail[:, 2:3] * (1.0 / 32768.0)
    total = spread(whole) * (jnp.exp2(spread(tail[:, 0:1]) - 15.0) * 2.0)
    return scales, total


def decode_blocks(read, scales, blocks, take):
    for scale, (low, high) in zip(scales, group_ranges(blocks)):
        for block in range(low, high, 2):
            values = widen(read(block * COLS))
            take(block, values[:COLS] * scale)
            take(block + 1, values[COLS:] * scale)


def start_kernel(shaped_ref, residual_ref, code_ref):
    blocks = shaped_ref.shape[0]
    partial = jnp.zeros((COLS, LANES), F32)
    for block in range(blocks):
        partial = partial + shaped_ref[block] * residual_ref[block]

    def write(row, value):
        code_ref[row : row + 2 * COLS, :] = value

    encode(lambda block: shaped_ref[block], blocks, partial, write)


def factor_kernel(first, last, peers, *refs):
    refs = list(refs)
    near_ref, ints_ref, code_ref, shaped_ref, precision_ref, tiles_ref, small_ref = refs[:7]
    refs = refs[7:]
    if not first:
        old_field_ref, old_direction_ref, old_gamma_ref = refs[:3]
        refs = refs[3:]
    out_ref, own_ref, direction_ref, gamma_ref = refs[:4]
    field_ref, running_ref, partial_ref, held_ref, semaphores = refs[4:]
    blocks = shaped_ref.shape[0]
    me, core = ints_ref[0], ints_ref[1]
    steps = tiles_ref.shape[0]
    step_blocks = blocks // steps
    half = step_blocks // 2
    slots = 4
    buffers = held_ref.shape[0]

    def fetch(step):
        buffer = lax.rem(step, buffers)
        return pltpu.make_async_copy(tiles_ref.at[step], held_ref.at[buffer], semaphores.at[buffer])

    for step in range(min(buffers, steps)):
        fetch(step).start()

    gamma = jnp.zeros((COLS, LANES), F32)
    for peer in range(peers):
        gamma = gamma + decode_tail(code_ref[peer, blocks * COLS :, :])[1]
    gamma_ref[...] = gamma
    if not first:
        beta = gamma / old_gamma_ref[...]

    def take(peer, carry):
        scales, unused = decode_tail(code_ref[peer, blocks * COLS :, :])

        def keep(block, values):
            place = peer * blocks + block
            if not first:
                values = values + beta * join_rows(old_field_ref[place].astype(F32))
            field_ref[place] = split_rows(values)
            running_ref[place] = jnp.zeros((COLS, LANES), F32)

        def read(row):
            return code_ref[peer, row : row + 2 * COLS, :]

        decode_blocks(read, scales, blocks, keep)
        return carry

    lax.fori_loop(0, peers, take, 0)
    for block in range(blocks):
        values = shaped_ref[block]
        if not first:
            values = values + beta * old_direction_ref[block]
        direction_ref[block] = values
    partial_ref[...] = jnp.zeros_like(partial_ref)

    def work(step, carry):
        fetch(step).wait()
        buffer = lax.rem(step, buffers)
        came = ints_ref[2 + step]

        def tile_row(inner):
            parts = [
                held_ref[buffer, part, inner * slots + slot]
                for part in range(2)
                for slot in range(slots)
            ]
            parts.append(small_ref[lax.rem(inner // half + core, 2), came, inner % half])
            return jnp.concatenate(parts, axis=1)

        partial = partial_ref[...]
        kept = []
        for inner in range(step_blocks):
            block = step * step_blocks + inner
            places = [near_ref[block * 2 * slots + k] for k in range(2 * slots)]
            left = [field_ref[place] for place in places] + [split_rows(direction_ref[block])]
            summed = join_rows(
                lax.dot_general(
                    jnp.concatenate(left, axis=1),
                    tile_row(inner),
                    (((1,), (1,)), ((), ())),
                    preferred_element_type=F32,
                )
            )
            weighted = precision_ref[pl.ds(block, 1), :] * summed
            partial = partial + weighted * summed
            kept.append((block, places, split_rows(weighted)))
        partial_ref[...] = partial
        for inner, (block, places, weighted) in enumerate(kept):
            pieces = join_rows(
                jnp.dot(weighted, tile_row(inner), preferred_element_type=F32)
            )
            own_ref[block] = pieces[:, 2 * slots * LANES :]
            for k, place in enumerate(places):
                running_ref[place] = running_ref[place] + pieces[:, k * LANES : (k + 1) * LANES]

        @pl.when(step + buffers < steps)
        def refill():
            fetch(step + buffers).start()

        return carry

    lax.fori_loop(0, steps, work, 0)

    for block in range(blocks):
        own_ref[block] = own_ref[block] + running_ref[me * blocks + block]

    def give(peer, carry):
        def write(row, value):
            out_ref[peer, row : row + 2 * COLS, :] = value

        encode(lambda block: running_ref[peer * blocks + block], blocks, partial_ref[...], write)
        return carry

    lax.fori_loop(0, peers, give, 0)


def update_kernel(last, peers, *refs):
    refs = list(refs)
    ints_ref, code_ref, own_ref, residual_ref, solution_ref, direction_ref, gamma_ref = refs[:7]
    refs = refs[7:]
    if last:
        new_residual_ref, new_solution_ref, image_ref = refs
    else:
        small_ref, new_residual_ref, new_solution_ref, shaped_ref, out_ref, image_ref = refs
    blocks = own_ref.shape[0]
    me, core = ints_ref[0], ints_ref[1]
    for block in range(blocks):
        image_ref[block] = own_ref[block]

    def take(peer, bottom):
        scales, total = decode_tail(code_ref[peer, blocks * COLS :, :])
        scales = [jnp.where(peer == me, 0.0, scale) for scale in scales]

        def read(row):
            return code_ref[peer, row : row + 2 * COLS, :]

        def add(block, values):
            image_ref[block] = image_ref[block] + values

        decode_blocks(read, scales, blocks, add)
        return bottom + total

    bottom = lax.fori_loop(0, peers, take, jnp.zeros((COLS, LANES), F32))
    alpha = gamma_ref[...] / bottom
    partial = jnp.zeros((COLS, LANES), F32)
    for block in range(blocks):
        new_solution_ref[block] = solution_ref[block] + alpha * direction_ref[block]
        residual = residual_ref[block] - alpha * image_ref[block]
        new_residual_ref[block] = residual
        if not last:
            half = small_ref.shape[2] // 2
            plane, inner = divmod(block, 2 * half)
            side = lax.rem(inner // half + core, 2)
            tile = small_ref[side, ints_ref[2 + plane], half + inner % half]
            shaped = join_rows(jnp.dot(split_rows(residual), tile, preferred_element_type=F32))
            shaped_ref[block] = shaped
            partial = partial + residual * shaped
    if not last:

        def write(row, value):
            out_ref[row : row + 2 * COLS, :] = value

        encode(lambda block: shaped_ref[block], blocks, partial, write)


WHOLE = pl.BlockSpec(memory_space=pltpu.VMEM)
SCALARS = pl.BlockSpec(memory_space=pltpu.SMEM)
PARAMS = pltpu.CompilerParams(vmem_limit_bytes=VMEM_LIMIT)


def start_call(shaped, residual):
    blocks = shaped.shape[0]
    return pl.pallas_call(
        start_kernel,
        out_shape=jax.ShapeDtypeStruct((blocks * COLS + EXTRA, LANES), I16),
        in_specs=[WHOLE, WHOLE],
        out_specs=WHOLE,
        compiler_params=PARAMS,
        name="start",
    )(shaped, residual)


def factor_call(first, last, near, ints, codes, shaped, precision, tiles, small, state):
    peers = codes.shape[0]
    blocks = shaped.shape[0]
    field = (peers * blocks, 2 * COLS, LANES)

    arguments = (near, ints, codes, shaped, precision, tiles, small, *state)
    outs = [
        (codes.shape, I16),
        (shaped.shape, F32),
        (shaped.shape, F32),
        ((COLS, LANES), F32),
    ]
    scratch = [
        pltpu.VMEM((peers * blocks, COLS, LANES), F32),
        pltpu.VMEM((COLS, LANES), F32),
        pltpu.VMEM((BUFFERS,) + tiles.shape[1:], BF16),
        pltpu.SemaphoreType.DMA((BUFFERS,)),
    ]
    if last:
        scratch = [pltpu.VMEM(field, BF16)] + scratch
    else:
        outs.append((field, BF16))
    return pl.pallas_call(
        lambda *refs: factor_kernel(first, last, peers, *refs),
        out_shape=[jax.ShapeDtypeStruct(*out) for out in outs],
        in_specs=[SCALARS] * 2
        + [WHOLE] * 3
        + [pl.BlockSpec(memory_space=pl.ANY)]
        + [WHOLE] * (len(arguments) - 6),
        out_specs=[WHOLE] * len(outs),
        scratch_shapes=scratch,
        compiler_params=PARAMS,
        name="factor",
    )(*arguments)


def update_call(last, ints, codes, own, residual, answer, direction, gamma, small):
    shape = jax.ShapeDtypeStruct(own.shape, F32)
    outs = [shape, shape]
    arguments = [ints, codes, own, residual, answer, direction, gamma]
    if not last:
        outs += [shape, jax.ShapeDtypeStruct(codes.shape[1:], I16)]
        arguments.append(small)
    return pl.pallas_call(
        lambda *refs: update_kernel(last, codes.shape[0], *refs),
        out_shape=outs,
        in_specs=[SCALARS] + [WHOLE] * (len(arguments) - 1),
        out_specs=[WHOLE] * len(outs),
        scratch_shapes=[pltpu.VMEM(own.shape, F32)],
        compiler_params=PARAMS,
        name="update",
    )(*arguments)


def shift(values, name, by):
    size = lax.axis_size(name)
    return lax.ppermute(values, name, [(index, (index + by) % size) for index in range(size)])


def local(right_side, diag_tiles, cond_tiles, neighbour_blocks, precision_diag, precond_tiles):
    depth, wide, high = (lax.axis_size(name) for name in ("z", "x", "y"))
    peers = wide * high
    here = right_side.shape[0]
    blocks = depth * here
    core = lax.axis_index("c")
    me = (lax.axis_index("x") * high + lax.axis_index("y")).astype(I32).reshape(1)
    half = here // 2

    tiles = lax.all_gather(cond_tiles.reshape(-1, LANES, LANES), ("z", "c"), axis=0, tiled=False)
    tiles = tiles.reshape((depth, 2, -1, LANES, LANES))

    place = lax.axis_index("z")
    halves = [
        lax.dynamic_slice_in_dim(values, core * half, half, 0)
        for values in (diag_tiles, precond_tiles)
    ]
    mine = jnp.concatenate(halves, axis=0)
    steps = (depth - 1) // 2
    ups, downs = [mine], [mine]
    offsets = [0]
    for step in range(1, steps + 1):
        ups.append(shift(ups[-1], "z", 1))
        downs.append(shift(downs[-1], "z", -1))
        offsets += [depth - step, step]
    offsets.append(depth // 2)
    middle = [shift(ups[-1][:half], "z", 1), shift(downs[-1][half:], "z", -1)]
    small = [mine]
    for up, down in zip(ups[1:], downs[1:]):
        small += [up, down]
    small = jnp.stack(small + [jnp.concatenate(middle, axis=0)])
    small = jnp.stack([small, shift(small, "c", 1)])
    order = np.argsort(np.asarray(offsets)).astype(np.int32)
    ahead = (jnp.arange(depth, dtype=I32) - place) % depth
    places = sum(jnp.where(ahead == offset, int(order[offset]), 0) for offset in range(depth))
    ints = jnp.concatenate([me, core.astype(I32).reshape(1), places.astype(I32)])

    wide_precond = precond_tiles.astype(F32)
    shaped = jnp.einsum("lts,lcs->lct", wide_precond, right_side, precision=lax.Precision.HIGHEST)
    near = jnp.pad(neighbour_blocks.astype(F32), ((0, 0), (0, LANES - neighbour_blocks.shape[1])))
    facts = jnp.concatenate([precision_diag, near], axis=0)
    facts = jnp.broadcast_to(facts[None], (depth,) + facts.shape)

    def by_column(values):
        values = values.reshape(here, depth, COLS, LANES).transpose(1, 0, 2, 3)
        return values.reshape(depth, here * COLS, LANES)

    sent = jnp.concatenate([by_column(right_side), by_column(shaped), facts], axis=1)
    came = lax.all_to_all(sent, "z", split_axis=0, concat_axis=0, tiled=True)
    rows = here * COLS
    residual = came[:, :rows].reshape(blocks, COLS, LANES)
    shaped = came[:, rows : 2 * rows].reshape(blocks, COLS, LANES)
    precision = came[:, 2 * rows : 2 * rows + here].reshape(blocks, LANES)
    near = came[:, 2 * rows + here :, : neighbour_blocks.shape[1]].astype(I32).reshape(-1)
    plane = near // (peers * here)
    near = (near // here) % peers * blocks + plane * here + near % here

    answer = jnp.zeros_like(residual)
    codes = start_call(shaped, residual)
    state = ()
    for iteration in range(ITERS):
        last = iteration + 1 == ITERS
        arrived = lax.all_gather(codes, ("x", "y"), axis=0, tiled=False)
        if iteration == 0:
            arrived, tiles, small = lax.optimization_barrier((arrived, tiles, small))
        leaving, own, direction, gamma, *field = factor_call(
            iteration == 0, last, near, ints, arrived, shaped, precision, tiles, small, state
        )
        terms = lax.all_to_all(leaving, ("x", "y"), split_axis=0, concat_axis=0, tiled=True)
        residual, answer, *rest = update_call(
            last, ints, terms, own, residual, answer, direction, gamma, small
        )
        if not last:
            shaped, codes = rest
            state = (field[0], direction, gamma)

    both = jnp.stack([answer, residual], axis=0).reshape(2, depth, here, COLS, LANES)
    both = lax.all_to_all(both, "z", split_axis=1, concat_axis=1, tiled=True)
    both = both.transpose(0, 2, 1, 3, 4).reshape(2, here, depth * COLS, LANES)
    return both[0], both[1]


def solution(mesh, dims=DIMS):
    grid = Mesh(np.asarray(mesh.devices).reshape(dims + (2,)), ("z", "x", "y", "c"))
    blk = ("z", "x", "y")
    return jax.shard_map(
        local,
        mesh=grid,
        in_specs=(P(blk, "c", None), P(blk), P(blk, "c"), P(blk), P(blk), P(blk)),
        out_specs=(P(blk, "c", None), P(blk, "c", None)),
        check_vma=False,
    )
```

```python
import jax
import jax.numpy as jnp
import numpy as np
from jax import lax
from jax.experimental import pallas as pl
from jax.experimental.pallas import tpu as pltpu
from jax.sharding import Mesh, PartitionSpec as P

ITERS = 3
DIMS = (8, 4, 4)
LANES = 128
COLS = 8
SHARE = 8
GROUPS = 3
EXTRA = (GROUPS + 1) * COLS
LOW_EXP = -100.0
F32, BF16, I16, I32 = jnp.float32, jnp.bfloat16, jnp.int16, jnp.int32
VMEM_LIMIT = 12 * 1024 * 1024


def spread(column):
    return jnp.broadcast_to(column, (column.shape[0], LANES))


def split_rows(values):
    lead = values.astype(BF16).astype(F32)
    return jnp.concatenate([lead, values - lead], axis=0).astype(BF16)


def join_rows(values):
    return values[:COLS] + values[COLS:]


def group_ranges(blocks):
    pairs = blocks // 2
    cuts = [2 * (pairs * part // GROUPS) for part in range(GROUPS + 1)]
    return list(zip(cuts[:-1], cuts[1:]))


def exponents(tops):
    exps = jnp.floor(jnp.log2(jnp.maximum(tops, 1e-35) * 1.0025)) + 1.0
    return jnp.clip(exps, LOW_EXP, 126.0)


def encode(read, blocks, partial, write):
    tail = []
    for low, high in group_ranges(blocks):
        tops = jnp.abs(read(low))
        for block in range(low + 1, high):
            tops = jnp.maximum(tops, jnp.abs(read(block)))
        exps = exponents(tops)
        tail.append(exps)
        scale = jnp.exp2(15.0 - exps)
        for block in range(low, high, 2):
            pair = jnp.concatenate([read(block) * scale, read(block + 1) * scale], axis=0)
            write(block * COLS, jnp.round(pair).astype(I32).astype(I16))
    total = spread(jnp.sum(partial, axis=1, keepdims=True))
    exps = exponents(jnp.abs(total))
    scaled = total * (jnp.exp2(15.0 - exps) * 0.5)
    first = jnp.round(scaled)
    second = jnp.round((scaled - first) * 32768.0)
    lane = lax.broadcasted_iota(I32, (COLS, LANES), 1)
    tail.append(jnp.where(lane == 0, exps, jnp.where(lane == 1, first, second)))
    for part in range(0, GROUPS + 1, 2):
        rows = jnp.concatenate(tail[part : part + 2], axis=0)
        write((blocks + part) * COLS, rows.astype(I32).astype(I16))


def widen(rows):
    return rows.astype(I32).astype(F32)


def decode_tail(rows):
    rows = widen(rows)
    scales = [jnp.exp2(rows[part * COLS : (part + 1) * COLS] - 15.0) for part in range(GROUPS)]
    tail = rows[GROUPS * COLS :]
    whole = tail[:, 1:2] + tail[:, 2:3] * (1.0 / 32768.0)
    total = spread(whole) * (jnp.exp2(spread(tail[:, 0:1]) - 15.0) * 2.0)
    return scales, total


def decode_blocks(read, scales, blocks, take):
    for scale, (low, high) in zip(scales, group_ranges(blocks)):
        for block in range(low, high, 2):
            values = widen(read(block * COLS))
            take(block, values[:COLS] * scale)
            take(block + 1, values[COLS:] * scale)


def start_kernel(shaped_ref, residual_ref, code_ref):
    blocks = shaped_ref.shape[0]
    partial = jnp.zeros((COLS, LANES), F32)
    for block in range(blocks):
        partial = partial + shaped_ref[block] * residual_ref[block]

    def write(row, value):
        code_ref[row : row + 2 * COLS, :] = value

    encode(lambda block: shaped_ref[block], blocks, partial, write)


def factor_kernel(first, last, peers, *refs):
    refs = list(refs)
    near_ref, me_ref, code_ref, shaped_ref, precision_ref, tiles_ref = refs[:6]
    refs = refs[6:]
    if not first:
        old_field_ref, old_direction_ref, old_gamma_ref = refs[:3]
        refs = refs[3:]
    out_ref, own_ref, direction_ref, gamma_ref = refs[:4]
    field_ref, running_ref, partial_ref = refs[4:]
    blocks = shaped_ref.shape[0]
    step_blocks = SHARE
    steps = blocks // step_blocks
    half = step_blocks // 2
    slots = 4

    def prologue():
        gamma = jnp.zeros((COLS, LANES), F32)
        for peer in range(peers):
            gamma = gamma + decode_tail(code_ref[peer, blocks * COLS :, :])[1]
        gamma_ref[...] = gamma
        if not first:
            beta = gamma / old_gamma_ref[...]

        def take(peer, carry):
            scales, unused = decode_tail(code_ref[peer, blocks * COLS :, :])

            def keep(block, values):
                place = peer * blocks + block
                if not first:
                    values = values + beta * join_rows(old_field_ref[place].astype(F32))
                field_ref[place] = split_rows(values)
                running_ref[place] = jnp.zeros((COLS, LANES), F32)

            def read(row):
                return code_ref[peer, row : row + 2 * COLS, :]

            decode_blocks(read, scales, blocks, keep)
            return carry

        lax.fori_loop(0, peers, take, 0)
        for block in range(blocks):
            values = shaped_ref[block]
            if not first:
                values = values + beta * old_direction_ref[block]
            direction_ref[block] = values
        partial_ref[...] = jnp.zeros_like(partial_ref)

    def work(step, at):
        def tile_row(inner):
            parts = [
                tiles_ref[at, core, inner * slots + slot]
                for core in range(2)
                for slot in range(slots)
            ]
            parts.append(tiles_ref[at, inner // half, slots * step_blocks + inner % half])
            return jnp.concatenate(parts, axis=1)

        partial = partial_ref[...]
        kept = []
        for inner in range(step_blocks):
            block = step * step_blocks + inner
            places = [near_ref[block * 2 * slots + k] for k in range(2 * slots)]
            left = [field_ref[place] for place in places] + [split_rows(direction_ref[block])]
            summed = join_rows(
                lax.dot_general(
                    jnp.concatenate(left, axis=1),
                    tile_row(inner),
                    (((1,), (1,)), ((), ())),
                    preferred_element_type=F32,
                )
            )
            weighted = precision_ref[pl.ds(block, 1), :] * summed
            partial = partial + weighted * summed
            kept.append((block, places, split_rows(weighted)))
        partial_ref[...] = partial
        for inner, (block, places, weighted) in enumerate(kept):
            pieces = join_rows(
                jnp.dot(weighted, tile_row(inner), preferred_element_type=F32)
            )
            own_ref[block] = pieces[:, 2 * slots * LANES :]
            for k, place in enumerate(places):
                running_ref[place] = running_ref[place] + pieces[:, k * LANES : (k + 1) * LANES]

    def epilogue():
        me = me_ref[0]
        for block in range(blocks):
            own_ref[block] = own_ref[block] + running_ref[me * blocks + block]

        def give(peer, carry):
            def write(row, value):
                out_ref[peer, row : row + 2 * COLS, :] = value

            encode(lambda block: running_ref[peer * blocks + block], blocks, partial_ref[...], write)
            return carry

        lax.fori_loop(0, peers, give, 0)

    def loop(step, carry):
        work(step, step)
        return carry

    prologue()
    lax.fori_loop(0, steps, loop, 0)
    epilogue()


def update_kernel(last, peers, *refs):
    refs = list(refs)
    me_ref, code_ref, own_ref, residual_ref, solution_ref, direction_ref, gamma_ref = refs[:7]
    refs = refs[7:]
    if last:
        out_ref, new_residual_ref, new_solution_ref, image_ref = refs
    else:
        precond_ref, new_residual_ref, new_solution_ref, shaped_ref, out_ref, image_ref = refs
    blocks = own_ref.shape[0]
    me = me_ref[0]
    for block in range(blocks):
        image_ref[block] = own_ref[block]

    def take(peer, bottom):
        scales, total = decode_tail(code_ref[peer, blocks * COLS :, :])
        scales = [jnp.where(peer == me, 0.0, scale) for scale in scales]

        def read(row):
            return code_ref[peer, row : row + 2 * COLS, :]

        def add(block, values):
            image_ref[block] = image_ref[block] + values

        decode_blocks(read, scales, blocks, add)
        return bottom + total

    bottom = lax.fori_loop(0, peers, take, jnp.zeros((COLS, LANES), F32))
    alpha = gamma_ref[...] / bottom
    partial = jnp.zeros((COLS, LANES), F32)
    for block in range(blocks):
        new_solution_ref[block] = solution_ref[block] + alpha * direction_ref[block]
        residual = residual_ref[block] - alpha * image_ref[block]
        new_residual_ref[block] = residual
        if not last:
            shaped = join_rows(
                jnp.dot(split_rows(residual), precond_ref[block], preferred_element_type=F32)
            )
            shaped_ref[block] = shaped
            partial = partial + residual * shaped
    if not last:

        def write(row, value):
            out_ref[row : row + 2 * COLS, :] = value

        encode(lambda block: shaped_ref[block], blocks, partial, write)
    else:
        for plane in range(blocks // SHARE):
            for part, ref in enumerate((new_solution_ref, new_residual_ref)):
                first = plane * SHARE
                tops = jnp.abs(ref[first])
                for inner in range(1, SHARE):
                    tops = jnp.maximum(tops, jnp.abs(ref[first + inner]))
                exps = exponents(tops)
                scale = jnp.exp2(15.0 - exps)
                for inner in range(0, SHARE, 2):
                    pair = jnp.concatenate(
                        [ref[first + inner] * scale, ref[first + inner + 1] * scale], axis=0
                    )
                    row = (part * SHARE + inner) * COLS
                    out_ref[plane, row : row + 2 * COLS, :] = jnp.round(pair).astype(I32).astype(I16)
                kept = exps if part == 0 else jnp.concatenate([kept, exps], axis=0)
            out_ref[plane, 2 * SHARE * COLS :, :] = kept.astype(I32).astype(I16)


def finish_kernel(code_ref, solution_ref, residual_ref):
    for plane in range(code_ref.shape[0]):
        scales = jnp.exp2(widen(code_ref[plane, 2 * SHARE * COLS :, :]) - 15.0)
        for part, ref in enumerate((solution_ref, residual_ref)):
            scale = scales[part * COLS : (part + 1) * COLS]
            for inner in range(0, SHARE, 2):
                row = (part * SHARE + inner) * COLS
                values = widen(code_ref[plane, row : row + 2 * COLS, :])
                columns = slice(plane * COLS, (plane + 1) * COLS)
                ref[inner, columns, :] = values[:COLS] * scale
                ref[inner + 1, columns, :] = values[COLS:] * scale


WHOLE = pl.BlockSpec(memory_space=pltpu.VMEM)
SCALARS = pl.BlockSpec(memory_space=pltpu.SMEM)
PARAMS = pltpu.CompilerParams(vmem_limit_bytes=VMEM_LIMIT)


def start_call(shaped, residual):
    blocks = shaped.shape[0]
    return pl.pallas_call(
        start_kernel,
        out_shape=jax.ShapeDtypeStruct((blocks * COLS + EXTRA, LANES), I16),
        in_specs=[WHOLE, WHOLE],
        out_specs=WHOLE,
        compiler_params=PARAMS,
        name="start",
    )(shaped, residual)


def factor_call(first, last, near, me, codes, shaped, precision, tiles, state):
    peers = codes.shape[0]
    blocks = shaped.shape[0]
    field = (peers * blocks, 2 * COLS, LANES)

    arguments = (near, me, codes, shaped, precision, tiles, *state)
    outs = [
        (codes.shape, I16),
        (shaped.shape, F32),
        (shaped.shape, F32),
        ((COLS, LANES), F32),
    ]
    scratch = [
        pltpu.VMEM((peers * blocks, COLS, LANES), F32),
        pltpu.VMEM((COLS, LANES), F32),
    ]
    if last:
        scratch = [pltpu.VMEM(field, BF16)] + scratch
    else:
        outs.append((field, BF16))
    return pl.pallas_call(
        lambda *refs: factor_kernel(first, last, peers, *refs),
        out_shape=[jax.ShapeDtypeStruct(*out) for out in outs],
        in_specs=[SCALARS] * 2 + [WHOLE] * (len(arguments) - 2),
        out_specs=[WHOLE] * len(outs),
        scratch_shapes=scratch,
        compiler_params=PARAMS,
        name="factor",
    )(*arguments)


def update_call(last, me, codes, own, residual, answer, direction, gamma, precond):
    shape = jax.ShapeDtypeStruct(own.shape, F32)
    arguments = [me, codes, own, residual, answer, direction, gamma]
    if last:
        rows = 2 * SHARE * COLS + 2 * COLS
        outs = [jax.ShapeDtypeStruct((own.shape[0] // SHARE, rows, LANES), I16)]
        scratch = [pltpu.VMEM(own.shape, F32)] * 3
    else:
        outs = [shape, shape, shape, jax.ShapeDtypeStruct(codes.shape[1:], I16)]
        scratch = [pltpu.VMEM(own.shape, F32)]
        arguments.append(precond)
    return pl.pallas_call(
        lambda *refs: update_kernel(last, codes.shape[0], *refs),
        out_shape=outs,
        in_specs=[SCALARS] + [WHOLE] * (len(arguments) - 1),
        out_specs=[WHOLE] * len(outs),
        scratch_shapes=scratch,
        compiler_params=PARAMS,
        name="update",
    )(*arguments)


def finish_call(codes):
    shape = jax.ShapeDtypeStruct((SHARE, codes.shape[0] * COLS, LANES), F32)
    return pl.pallas_call(
        finish_kernel,
        out_shape=[shape, shape],
        in_specs=[WHOLE],
        out_specs=[WHOLE, WHOLE],
        compiler_params=PARAMS,
        name="finish",
    )(codes)


def local(right_side, diag_tiles, cond_tiles, neighbour_blocks, precision_diag, precond_tiles):
    depth, wide, high = (lax.axis_size(name) for name in ("z", "x", "y"))
    peers = wide * high
    here = right_side.shape[0]
    blocks = depth * here
    core = lax.axis_index("c")
    me = (lax.axis_index("x") * high + lax.axis_index("y")).astype(I32).reshape(1)
    half = here // 2

    own_diag = lax.dynamic_slice_in_dim(diag_tiles, core * half, half, 0)
    mine = jnp.concatenate([cond_tiles.reshape(-1, LANES, LANES), own_diag], axis=0)
    tiles = lax.all_gather(mine, ("z", "c"), axis=0, tiled=False)
    tiles = tiles.reshape((depth, 2) + mine.shape)
    own_precond = lax.dynamic_slice_in_dim(precond_tiles, core * half, half, 0)

    wide_precond = precond_tiles.astype(F32)
    shaped = jnp.einsum("lts,lcs->lct", wide_precond, right_side, precision=lax.Precision.HIGHEST)
    near = jnp.pad(neighbour_blocks.astype(F32), ((0, 0), (0, LANES - neighbour_blocks.shape[1])))
    facts = jnp.concatenate([precision_diag, near], axis=0)
    facts = jnp.broadcast_to(facts[None], (depth,) + facts.shape)

    def by_column(values):
        values = values.reshape(here, depth, COLS, LANES).transpose(1, 0, 2, 3)
        return values.reshape(depth, here * COLS, LANES)

    sent = jnp.concatenate([by_column(right_side), by_column(shaped), facts], axis=1)
    came = lax.all_to_all(sent, "z", split_axis=0, concat_axis=0, tiled=True)
    rows = here * COLS
    residual = came[:, :rows].reshape(blocks, COLS, LANES)
    shaped = came[:, rows : 2 * rows].reshape(blocks, COLS, LANES)
    precision = came[:, 2 * rows : 2 * rows + here].reshape(blocks, LANES)
    near = came[:, 2 * rows + here :, : neighbour_blocks.shape[1]].astype(I32).reshape(-1)
    plane = near // (peers * here)
    near = (near // here) % peers * blocks + plane * here + near % here

    answer = jnp.zeros_like(residual)
    codes = start_call(shaped, residual)
    state = ()
    for iteration in range(ITERS):
        last = iteration + 1 == ITERS
        arrived = lax.all_gather(codes, ("x", "y"), axis=0, tiled=False)
        if iteration == 0:
            arrived, near, precision, tiles, own_precond = lax.optimization_barrier(
                (arrived, near, precision, tiles, own_precond)
            )
            precond = lax.all_gather(own_precond, ("z", "c"), axis=0, tiled=True)
        leaving, own, direction, gamma, *field = factor_call(
            iteration == 0, last, near, me, arrived, shaped, precision, tiles, state
        )
        terms = lax.all_to_all(leaving, ("x", "y"), split_axis=0, concat_axis=0, tiled=True)
        results = update_call(
            last, me, terms, own, residual, answer, direction, gamma, precond
        )
        if not last:
            residual, answer, shaped, codes = results
            state = (field[0], direction, gamma)

    codes = lax.all_to_all(results[0], "z", split_axis=0, concat_axis=0, tiled=True)
    answer, residual = finish_call(codes)
    return answer, residual


def solution(mesh, dims=DIMS):
    grid = Mesh(np.asarray(mesh.devices).reshape(dims + (2,)), ("z", "x", "y", "c"))
    blk = ("z", "x", "y")
    return jax.shard_map(
        local,
        mesh=grid,
        in_specs=(P(blk, "c", None), P(blk), P(blk, "c"), P(blk), P(blk), P(blk)),
        out_specs=(P(blk, "c", None), P(blk, "c", None)),
        check_vma=False,
    )
```

```python
import jax
import jax.numpy as jnp
import numpy as np
from jax import lax
from jax.experimental import pallas as pl
from jax.experimental.pallas import tpu as pltpu
from jax.sharding import Mesh, PartitionSpec as P

ITERS = 3
DIMS = (8, 4, 4)
LANES = 128
COLS = 8
SHARE = 8
GROUPS = 3
EXTRA = (GROUPS + 1) * COLS
BUFFERS = 8
LOW_EXP = -100.0
F32, BF16, I16, I32 = jnp.float32, jnp.bfloat16, jnp.int16, jnp.int32
VMEM_LIMIT = 12 * 1024 * 1024
STREAM_LIMIT = 46 * 1024 * 1024


def spread(column):
    return jnp.broadcast_to(column, (column.shape[0], LANES))


def split_rows(values):
    lead = values.astype(BF16).astype(F32)
    return jnp.concatenate([lead, values - lead], axis=0).astype(BF16)


def join_rows(values):
    return values[:COLS] + values[COLS:]


def group_ranges(blocks):
    pairs = blocks // 2
    cuts = [2 * (pairs * part // GROUPS) for part in range(GROUPS + 1)]
    return list(zip(cuts[:-1], cuts[1:]))


def exponents(tops):
    exps = jnp.floor(jnp.log2(jnp.maximum(tops, 1e-35) * 1.0025)) + 1.0
    return jnp.clip(exps, LOW_EXP, 126.0)


def encode(read, blocks, partial, write):
    tail = []
    for low, high in group_ranges(blocks):
        tops = jnp.abs(read(low))
        for block in range(low + 1, high):
            tops = jnp.maximum(tops, jnp.abs(read(block)))
        exps = exponents(tops)
        tail.append(exps)
        scale = jnp.exp2(15.0 - exps)
        for block in range(low, high, 2):
            pair = jnp.concatenate([read(block) * scale, read(block + 1) * scale], axis=0)
            write(block * COLS, jnp.round(pair).astype(I32).astype(I16))
    total = spread(jnp.sum(partial, axis=1, keepdims=True))
    exps = exponents(jnp.abs(total))
    scaled = total * (jnp.exp2(15.0 - exps) * 0.5)
    first = jnp.round(scaled)
    second = jnp.round((scaled - first) * 32768.0)
    lane = lax.broadcasted_iota(I32, (COLS, LANES), 1)
    tail.append(jnp.where(lane == 0, exps, jnp.where(lane == 1, first, second)))
    for part in range(0, GROUPS + 1, 2):
        rows = jnp.concatenate(tail[part : part + 2], axis=0)
        write((blocks + part) * COLS, rows.astype(I32).astype(I16))


def widen(rows):
    return rows.astype(I32).astype(F32)


def decode_tail(rows):
    rows = widen(rows)
    scales = [jnp.exp2(rows[part * COLS : (part + 1) * COLS] - 15.0) for part in range(GROUPS)]
    tail = rows[GROUPS * COLS :]
    whole = tail[:, 1:2] + tail[:, 2:3] * (1.0 / 32768.0)
    total = spread(whole) * (jnp.exp2(spread(tail[:, 0:1]) - 15.0) * 2.0)
    return scales, total


def decode_blocks(read, scales, blocks, take):
    for scale, (low, high) in zip(scales, group_ranges(blocks)):
        for block in range(low, high, 2):
            values = widen(read(block * COLS))
            take(block, values[:COLS] * scale)
            take(block + 1, values[COLS:] * scale)


def start_kernel(shaped_ref, residual_ref, code_ref):
    blocks = shaped_ref.shape[0]
    partial = jnp.zeros((COLS, LANES), F32)
    for block in range(blocks):
        partial = partial + shaped_ref[block] * residual_ref[block]

    def write(row, value):
        code_ref[row : row + 2 * COLS, :] = value

    encode(lambda block: shaped_ref[block], blocks, partial, write)


def factor_kernel(first, last, peers, *refs):
    refs = list(refs)
    near_ref, me_ref, code_ref, shaped_ref, precision_ref, tiles_ref = refs[:6]
    refs = refs[6:]
    if not first:
        old_field_ref, old_direction_ref, old_gamma_ref = refs[:3]
        refs = refs[3:]
    out_ref, own_ref, direction_ref, gamma_ref = refs[:4]
    field_ref, running_ref, partial_ref, held_ref, semaphores = refs[4:]
    blocks = shaped_ref.shape[0]
    step_blocks = SHARE
    steps = blocks // step_blocks
    half = step_blocks // 2
    slots = 4
    buffers = held_ref.shape[0]

    def fetch(step):
        buffer = lax.rem(step, buffers)
        return pltpu.make_async_copy(tiles_ref.at[step], held_ref.at[buffer], semaphores.at[buffer])

    for step in range(min(buffers, steps)):
        fetch(step).start()

    def prologue():
        gamma = jnp.zeros((COLS, LANES), F32)
        for peer in range(peers):
            gamma = gamma + decode_tail(code_ref[peer, blocks * COLS :, :])[1]
        gamma_ref[...] = gamma
        if not first:
            beta = gamma / old_gamma_ref[...]

        def take(peer, carry):
            scales, unused = decode_tail(code_ref[peer, blocks * COLS :, :])

            def keep(block, values):
                place = peer * blocks + block
                if not first:
                    values = values + beta * join_rows(old_field_ref[place].astype(F32))
                field_ref[place] = split_rows(values)
                running_ref[place] = jnp.zeros((COLS, LANES), F32)

            def read(row):
                return code_ref[peer, row : row + 2 * COLS, :]

            decode_blocks(read, scales, blocks, keep)
            return carry

        lax.fori_loop(0, peers, take, 0)
        for block in range(blocks):
            values = shaped_ref[block]
            if not first:
                values = values + beta * old_direction_ref[block]
            direction_ref[block] = values
        partial_ref[...] = jnp.zeros_like(partial_ref)

    def work(step, at):
        def tile_row(inner):
            parts = [
                held_ref[at, core, inner * slots + slot]
                for core in range(2)
                for slot in range(slots)
            ]
            parts.append(held_ref[at, inner // half, slots * step_blocks + inner % half])
            return jnp.concatenate(parts, axis=1)

        partial = partial_ref[...]
        kept = []
        for inner in range(step_blocks):
            block = step * step_blocks + inner
            places = [near_ref[block * 2 * slots + k] for k in range(2 * slots)]
            left = [field_ref[place] for place in places] + [split_rows(direction_ref[block])]
            summed = join_rows(
                lax.dot_general(
                    jnp.concatenate(left, axis=1),
                    tile_row(inner),
                    (((1,), (1,)), ((), ())),
                    preferred_element_type=F32,
                )
            )
            weighted = precision_ref[pl.ds(block, 1), :] * summed
            partial = partial + weighted * summed
            kept.append((block, places, split_rows(weighted)))
        partial_ref[...] = partial
        for inner, (block, places, weighted) in enumerate(kept):
            pieces = join_rows(
                jnp.dot(weighted, tile_row(inner), preferred_element_type=F32)
            )
            own_ref[block] = pieces[:, 2 * slots * LANES :]
            for k, place in enumerate(places):
                running_ref[place] = running_ref[place] + pieces[:, k * LANES : (k + 1) * LANES]

    def epilogue():
        me = me_ref[0]
        for block in range(blocks):
            own_ref[block] = own_ref[block] + running_ref[me * blocks + block]

        def give(peer, carry):
            def write(row, value):
                out_ref[peer, row : row + 2 * COLS, :] = value

            encode(lambda block: running_ref[peer * blocks + block], blocks, partial_ref[...], write)
            return carry

        lax.fori_loop(0, peers, give, 0)

    def loop(step, carry):
        fetch(step).wait()
        work(step, lax.rem(step, buffers))

        @pl.when(step + buffers < steps)
        def refill():
            fetch(step + buffers).start()

        return carry

    prologue()
    lax.fori_loop(0, steps, loop, 0)
    epilogue()


def update_kernel(last, peers, *refs):
    refs = list(refs)
    me_ref, code_ref, own_ref, residual_ref, solution_ref, direction_ref, gamma_ref = refs[:7]
    refs = refs[7:]
    if last:
        out_ref, new_residual_ref, new_solution_ref, image_ref = refs
    else:
        precond_ref, new_residual_ref, new_solution_ref, shaped_ref, out_ref, image_ref = refs
    blocks = own_ref.shape[0]
    me = me_ref[0]
    for block in range(blocks):
        image_ref[block] = own_ref[block]

    def take(peer, bottom):
        scales, total = decode_tail(code_ref[peer, blocks * COLS :, :])
        scales = [jnp.where(peer == me, 0.0, scale) for scale in scales]

        def read(row):
            return code_ref[peer, row : row + 2 * COLS, :]

        def add(block, values):
            image_ref[block] = image_ref[block] + values

        decode_blocks(read, scales, blocks, add)
        return bottom + total

    bottom = lax.fori_loop(0, peers, take, jnp.zeros((COLS, LANES), F32))
    alpha = gamma_ref[...] / bottom
    partial = jnp.zeros((COLS, LANES), F32)
    for block in range(blocks):
        new_solution_ref[block] = solution_ref[block] + alpha * direction_ref[block]
        residual = residual_ref[block] - alpha * image_ref[block]
        new_residual_ref[block] = residual
        if not last:
            shaped = join_rows(
                jnp.dot(split_rows(residual), precond_ref[block], preferred_element_type=F32)
            )
            shaped_ref[block] = shaped
            partial = partial + residual * shaped
    if not last:

        def write(row, value):
            out_ref[row : row + 2 * COLS, :] = value

        encode(lambda block: shaped_ref[block], blocks, partial, write)
    else:
        for plane in range(blocks // SHARE):
            for part, ref in enumerate((new_solution_ref, new_residual_ref)):
                first = plane * SHARE
                tops = jnp.abs(ref[first])
                for inner in range(1, SHARE):
                    tops = jnp.maximum(tops, jnp.abs(ref[first + inner]))
                exps = exponents(tops)
                scale = jnp.exp2(15.0 - exps)
                for inner in range(0, SHARE, 2):
                    pair = jnp.concatenate(
                        [ref[first + inner] * scale, ref[first + inner + 1] * scale], axis=0
                    )
                    row = (part * SHARE + inner) * COLS
                    out_ref[plane, row : row + 2 * COLS, :] = jnp.round(pair).astype(I32).astype(I16)
                kept = exps if part == 0 else jnp.concatenate([kept, exps], axis=0)
            out_ref[plane, 2 * SHARE * COLS :, :] = kept.astype(I32).astype(I16)


def finish_kernel(code_ref, solution_ref, residual_ref):
    for plane in range(code_ref.shape[0]):
        scales = jnp.exp2(widen(code_ref[plane, 2 * SHARE * COLS :, :]) - 15.0)
        for part, ref in enumerate((solution_ref, residual_ref)):
            scale = scales[part * COLS : (part + 1) * COLS]
            for inner in range(0, SHARE, 2):
                row = (part * SHARE + inner) * COLS
                values = widen(code_ref[plane, row : row + 2 * COLS, :])
                columns = slice(plane * COLS, (plane + 1) * COLS)
                ref[inner, columns, :] = values[:COLS] * scale
                ref[inner + 1, columns, :] = values[COLS:] * scale


WHOLE = pl.BlockSpec(memory_space=pltpu.VMEM)
SCALARS = pl.BlockSpec(memory_space=pltpu.SMEM)
PARAMS = pltpu.CompilerParams(vmem_limit_bytes=VMEM_LIMIT)


def start_call(shaped, residual):
    blocks = shaped.shape[0]
    return pl.pallas_call(
        start_kernel,
        out_shape=jax.ShapeDtypeStruct((blocks * COLS + EXTRA, LANES), I16),
        in_specs=[WHOLE, WHOLE],
        out_specs=WHOLE,
        compiler_params=PARAMS,
        name="start",
    )(shaped, residual)


def factor_call(first, last, near, me, codes, shaped, precision, tiles, state):
    peers = codes.shape[0]
    blocks = shaped.shape[0]
    field = (peers * blocks, 2 * COLS, LANES)

    arguments = (near, me, codes, shaped, precision, tiles, *state)
    outs = [
        (codes.shape, I16),
        (shaped.shape, F32),
        (shaped.shape, F32),
        ((COLS, LANES), F32),
    ]
    scratch = [
        pltpu.VMEM((peers * blocks, COLS, LANES), F32),
        pltpu.VMEM((COLS, LANES), F32),
        pltpu.VMEM((BUFFERS,) + tiles.shape[1:], BF16),
        pltpu.SemaphoreType.DMA((BUFFERS,)),
    ]
    if last:
        scratch = [pltpu.VMEM(field, BF16)] + scratch
    else:
        outs.append((field, BF16))
    return pl.pallas_call(
        lambda *refs: factor_kernel(first, last, peers, *refs),
        out_shape=[jax.ShapeDtypeStruct(*out) for out in outs],
        in_specs=[SCALARS] * 2
        + [WHOLE] * 3
        + [pl.BlockSpec(memory_space=pl.ANY)]
        + [WHOLE] * (len(arguments) - 6),
        out_specs=[WHOLE] * len(outs),
        scratch_shapes=scratch,
        compiler_params=pltpu.CompilerParams(vmem_limit_bytes=STREAM_LIMIT),
        name="factor",
    )(*arguments)


def update_call(last, me, codes, own, residual, answer, direction, gamma, precond):
    shape = jax.ShapeDtypeStruct(own.shape, F32)
    arguments = [me, codes, own, residual, answer, direction, gamma]
    if last:
        rows = 2 * SHARE * COLS + 2 * COLS
        outs = [jax.ShapeDtypeStruct((own.shape[0] // SHARE, rows, LANES), I16)]
        scratch = [pltpu.VMEM(own.shape, F32)] * 3
    else:
        outs = [shape, shape, shape, jax.ShapeDtypeStruct(codes.shape[1:], I16)]
        scratch = [pltpu.VMEM(own.shape, F32)]
        arguments.append(precond)
    in_specs = [SCALARS] + [WHOLE] * (len(arguments) - 1)
    return pl.pallas_call(
        lambda *refs: update_kernel(last, codes.shape[0], *refs),
        out_shape=outs,
        in_specs=in_specs,
        out_specs=[WHOLE] * len(outs),
        scratch_shapes=scratch,
        compiler_params=PARAMS,
        name="update",
    )(*arguments)


def finish_call(codes):
    shape = jax.ShapeDtypeStruct((SHARE, codes.shape[0] * COLS, LANES), F32)
    return pl.pallas_call(
        finish_kernel,
        out_shape=[shape, shape],
        in_specs=[WHOLE],
        out_specs=[WHOLE, WHOLE],
        compiler_params=PARAMS,
        name="finish",
    )(codes)


def local(right_side, diag_tiles, cond_tiles, neighbour_blocks, precision_diag, precond_tiles):
    depth, wide, high = (lax.axis_size(name) for name in ("z", "x", "y"))
    peers = wide * high
    here = right_side.shape[0]
    blocks = depth * here
    core = lax.axis_index("c")
    me = (lax.axis_index("x") * high + lax.axis_index("y")).astype(I32).reshape(1)
    half = here // 2

    own_diag = lax.dynamic_slice_in_dim(diag_tiles, core * half, half, 0)
    mine = jnp.concatenate([cond_tiles.reshape(-1, LANES, LANES), own_diag], axis=0)
    tiles = lax.all_gather(mine, ("z", "c"), axis=0, tiled=False)
    tiles = tiles.reshape((depth, 2) + mine.shape)
    own_precond = lax.dynamic_slice_in_dim(precond_tiles, core * half, half, 0)

    wide_precond = precond_tiles.astype(F32)
    shaped = jnp.einsum("lts,lcs->lct", wide_precond, right_side, precision=lax.Precision.HIGHEST)
    near = jnp.pad(neighbour_blocks.astype(F32), ((0, 0), (0, LANES - neighbour_blocks.shape[1])))
    facts = jnp.concatenate([precision_diag, near], axis=0)
    facts = jnp.broadcast_to(facts[None], (depth,) + facts.shape)

    def by_column(values):
        values = values.reshape(here, depth, COLS, LANES).transpose(1, 0, 2, 3)
        return values.reshape(depth, here * COLS, LANES)

    sent = jnp.concatenate([by_column(right_side), by_column(shaped), facts], axis=1)
    came = lax.all_to_all(sent, "z", split_axis=0, concat_axis=0, tiled=True)
    rows = here * COLS
    residual = came[:, :rows].reshape(blocks, COLS, LANES)
    shaped = came[:, rows : 2 * rows].reshape(blocks, COLS, LANES)
    precision = came[:, 2 * rows : 2 * rows + here].reshape(blocks, LANES)
    near = came[:, 2 * rows + here :, : neighbour_blocks.shape[1]].astype(I32).reshape(-1)
    plane = near // (peers * here)
    near = (near // here) % peers * blocks + plane * here + near % here

    answer = jnp.zeros_like(residual)
    codes = start_call(shaped, residual)
    state = ()
    for iteration in range(ITERS):
        last = iteration + 1 == ITERS
        arrived = lax.all_gather(codes, ("x", "y"), axis=0, tiled=False)
        if iteration == 0:
            arrived, near, precision, tiles, own_precond = lax.optimization_barrier(
                (arrived, near, precision, tiles, own_precond)
            )
            precond = lax.all_gather(own_precond, ("z", "c"), axis=0, tiled=True)
        leaving, own, direction, gamma, *field = factor_call(
            iteration == 0, last, near, me, arrived, shaped, precision, tiles, state
        )
        terms = lax.all_to_all(leaving, ("x", "y"), split_axis=0, concat_axis=0, tiled=True)
        results = update_call(
            last, me, terms, own, residual, answer, direction, gamma, precond
        )
        if not last:
            residual, answer, shaped, codes = results
            state = (field[0], direction, gamma)

    codes = lax.all_to_all(results[0], "z", split_axis=0, concat_axis=0, tiled=True)
    answer, residual = finish_call(codes)
    return answer, residual


def solution(mesh, dims=DIMS):
    grid = Mesh(np.asarray(mesh.devices).reshape(dims + (2,)), ("z", "x", "y", "c"))
    blk = ("z", "x", "y")
    return jax.shard_map(
        local,
        mesh=grid,
        in_specs=(P(blk, "c", None), P(blk), P(blk, "c"), P(blk), P(blk), P(blk)),
        out_specs=(P(blk, "c", None), P(blk, "c", None)),
        check_vma=False,
    )
```

```python
import jax
import jax.numpy as jnp
import numpy as np
from jax import lax
from jax.experimental import pallas as pl
from jax.experimental.pallas import tpu as pltpu
from jax.sharding import Mesh, PartitionSpec as P

ITERS = 3
DIMS = (8, 4, 4)
LANES = 128
COLS = 8
SHARE = 8
GROUPS = 3
EXTRA = (GROUPS + 1) * COLS
BUFFERS = 8
LOW_EXP = -100.0
F32, BF16, I16, I32 = jnp.float32, jnp.bfloat16, jnp.int16, jnp.int32
VMEM_LIMIT = 12 * 1024 * 1024
STREAM_LIMIT = 38 * 1024 * 1024


def spread(column):
    return jnp.broadcast_to(column, (column.shape[0], LANES))


def split_rows(values):
    lead = values.astype(BF16).astype(F32)
    return jnp.concatenate([lead, values - lead], axis=0).astype(BF16)


def join_rows(values):
    return values[:COLS] + values[COLS:]


def group_ranges(blocks):
    pairs = blocks // 2
    cuts = [2 * (pairs * part // GROUPS) for part in range(GROUPS + 1)]
    return list(zip(cuts[:-1], cuts[1:]))


def exponents(tops):
    exps = jnp.floor(jnp.log2(jnp.maximum(tops, 1e-35) * 1.0025)) + 1.0
    return jnp.clip(exps, LOW_EXP, 126.0)


def encode(read, blocks, partial, write):
    tail = []
    for low, high in group_ranges(blocks):
        tops = jnp.abs(read(low))
        for block in range(low + 1, high):
            tops = jnp.maximum(tops, jnp.abs(read(block)))
        exps = exponents(tops)
        tail.append(exps)
        scale = jnp.exp2(15.0 - exps)
        for block in range(low, high, 2):
            pair = jnp.concatenate([read(block) * scale, read(block + 1) * scale], axis=0)
            write(block * COLS, jnp.round(pair).astype(I32).astype(I16))
    total = spread(jnp.sum(partial, axis=1, keepdims=True))
    exps = exponents(jnp.abs(total))
    scaled = total * (jnp.exp2(15.0 - exps) * 0.5)
    first = jnp.round(scaled)
    second = jnp.round((scaled - first) * 32768.0)
    lane = lax.broadcasted_iota(I32, (COLS, LANES), 1)
    tail.append(jnp.where(lane == 0, exps, jnp.where(lane == 1, first, second)))
    for part in range(0, GROUPS + 1, 2):
        rows = jnp.concatenate(tail[part : part + 2], axis=0)
        write((blocks + part) * COLS, rows.astype(I32).astype(I16))


def widen(rows):
    return rows.astype(I32).astype(F32)


def decode_tail(rows):
    rows = widen(rows)
    scales = [jnp.exp2(rows[part * COLS : (part + 1) * COLS] - 15.0) for part in range(GROUPS)]
    tail = rows[GROUPS * COLS :]
    whole = tail[:, 1:2] + tail[:, 2:3] * (1.0 / 32768.0)
    total = spread(whole) * (jnp.exp2(spread(tail[:, 0:1]) - 15.0) * 2.0)
    return scales, total


def decode_blocks(read, scales, blocks, take):
    for scale, (low, high) in zip(scales, group_ranges(blocks)):
        for block in range(low, high, 2):
            values = widen(read(block * COLS))
            take(block, values[:COLS] * scale)
            take(block + 1, values[COLS:] * scale)


def start_kernel(shaped_ref, residual_ref, code_ref):
    blocks = shaped_ref.shape[0]
    partial = jnp.zeros((COLS, LANES), F32)
    for block in range(blocks):
        partial = partial + shaped_ref[block] * residual_ref[block]

    def write(row, value):
        code_ref[row : row + 2 * COLS, :] = value

    encode(lambda block: shaped_ref[block], blocks, partial, write)


def factor_kernel(first, last, peers, *refs):
    refs = list(refs)
    near_ref, me_ref, code_ref, shaped_ref, precision_ref, tiles_ref = refs[:6]
    refs = refs[6:]
    if not first:
        old_field_ref, old_direction_ref, old_gamma_ref = refs[:3]
        refs = refs[3:]
    out_ref, own_ref, direction_ref, gamma_ref = refs[:4]
    field_ref, running_ref, partial_ref, held_ref, semaphores = refs[4:]
    blocks = shaped_ref.shape[0]
    step_blocks = SHARE
    steps = blocks // step_blocks
    half = step_blocks // 2
    slots = 4
    buffers = held_ref.shape[0]

    def fetch(step):
        buffer = lax.rem(step, buffers)
        return pltpu.make_async_copy(tiles_ref.at[step], held_ref.at[buffer], semaphores.at[buffer])

    for step in range(min(buffers, steps)):
        fetch(step).start()

    def prologue():
        gamma = jnp.zeros((COLS, LANES), F32)
        for peer in range(peers):
            gamma = gamma + decode_tail(code_ref[peer, blocks * COLS :, :])[1]
        gamma_ref[...] = gamma
        if not first:
            beta = gamma / old_gamma_ref[...]

        def take(peer, carry):
            scales, unused = decode_tail(code_ref[peer, blocks * COLS :, :])

            def keep(block, values):
                place = peer * blocks + block
                if not first:
                    values = values + beta * join_rows(old_field_ref[place].astype(F32))
                field_ref[place] = split_rows(values)
                running_ref[place] = jnp.zeros((COLS, LANES), F32)

            def read(row):
                return code_ref[peer, row : row + 2 * COLS, :]

            decode_blocks(read, scales, blocks, keep)
            return carry

        lax.fori_loop(0, peers, take, 0)
        for block in range(blocks):
            values = shaped_ref[block]
            if not first:
                values = values + beta * old_direction_ref[block]
            direction_ref[block] = values
        partial_ref[...] = jnp.zeros_like(partial_ref)

    def work(step, at):
        def tile_row(inner):
            parts = [
                held_ref[at, core, inner * slots + slot]
                for core in range(2)
                for slot in range(slots)
            ]
            parts.append(held_ref[at, inner // half, slots * step_blocks + inner % half])
            return jnp.concatenate(parts, axis=1)

        partial = partial_ref[...]
        kept = []
        for inner in range(step_blocks):
            block = step * step_blocks + inner
            places = [near_ref[block * 2 * slots + k] for k in range(2 * slots)]
            left = [field_ref[place] for place in places] + [split_rows(direction_ref[block])]
            summed = join_rows(
                lax.dot_general(
                    jnp.concatenate(left, axis=1),
                    tile_row(inner),
                    (((1,), (1,)), ((), ())),
                    preferred_element_type=F32,
                )
            )
            weighted = precision_ref[pl.ds(block, 1), :] * summed
            partial = partial + weighted * summed
            kept.append((block, places, split_rows(weighted)))
        partial_ref[...] = partial
        for inner, (block, places, weighted) in enumerate(kept):
            pieces = join_rows(
                jnp.dot(weighted, tile_row(inner), preferred_element_type=F32)
            )
            own_ref[block] = pieces[:, 2 * slots * LANES :]
            for k, place in enumerate(places):
                running_ref[place] = running_ref[place] + pieces[:, k * LANES : (k + 1) * LANES]

    def epilogue():
        me = me_ref[0]
        for block in range(blocks):
            own_ref[block] = own_ref[block] + running_ref[me * blocks + block]

        def give(peer, carry):
            def write(row, value):
                out_ref[peer, row : row + 2 * COLS, :] = value

            encode(lambda block: running_ref[peer * blocks + block], blocks, partial_ref[...], write)
            return carry

        lax.fori_loop(0, peers, give, 0)

    def loop(step, carry):
        fetch(step).wait()
        work(step, lax.rem(step, buffers))

        @pl.when(step + buffers < steps)
        def refill():
            fetch(step + buffers).start()

        return carry

    prologue()
    lax.fori_loop(0, steps, loop, 0)
    epilogue()


def update_kernel(last, peers, *refs):
    refs = list(refs)
    me_ref, code_ref, own_ref, residual_ref, solution_ref, direction_ref, gamma_ref = refs[:7]
    refs = refs[7:]
    if last:
        out_ref, new_residual_ref, new_solution_ref, image_ref = refs
    else:
        precond_ref, new_residual_ref, new_solution_ref, shaped_ref, out_ref, image_ref = refs
    blocks = own_ref.shape[0]
    me = me_ref[0]
    for block in range(blocks):
        image_ref[block] = own_ref[block]

    def take(peer, bottom):
        scales, total = decode_tail(code_ref[peer, blocks * COLS :, :])
        scales = [jnp.where(peer == me, 0.0, scale) for scale in scales]

        def read(row):
            return code_ref[peer, row : row + 2 * COLS, :]

        def add(block, values):
            image_ref[block] = image_ref[block] + values

        decode_blocks(read, scales, blocks, add)
        return bottom + total

    bottom = lax.fori_loop(0, peers, take, jnp.zeros((COLS, LANES), F32))
    alpha = gamma_ref[...] / bottom
    partial = jnp.zeros((COLS, LANES), F32)
    for block in range(blocks):
        new_solution_ref[block] = solution_ref[block] + alpha * direction_ref[block]
        residual = residual_ref[block] - alpha * image_ref[block]
        new_residual_ref[block] = residual
        if not last:
            shaped = join_rows(
                jnp.dot(split_rows(residual), precond_ref[block], preferred_element_type=F32)
            )
            shaped_ref[block] = shaped
            partial = partial + residual * shaped
    if not last:

        def write(row, value):
            out_ref[row : row + 2 * COLS, :] = value

        encode(lambda block: shaped_ref[block], blocks, partial, write)
    else:
        for plane in range(blocks // SHARE):
            for part, ref in enumerate((new_solution_ref, new_residual_ref)):
                first = plane * SHARE
                tops = jnp.abs(ref[first])
                for inner in range(1, SHARE):
                    tops = jnp.maximum(tops, jnp.abs(ref[first + inner]))
                exps = exponents(tops)
                scale = jnp.exp2(15.0 - exps)
                for inner in range(0, SHARE, 2):
                    pair = jnp.concatenate(
                        [ref[first + inner] * scale, ref[first + inner + 1] * scale], axis=0
                    )
                    row = (part * SHARE + inner) * COLS
                    out_ref[plane, row : row + 2 * COLS, :] = jnp.round(pair).astype(I32).astype(I16)
                kept = exps if part == 0 else jnp.concatenate([kept, exps], axis=0)
            out_ref[plane, 2 * SHARE * COLS :, :] = kept.astype(I32).astype(I16)


def finish_kernel(code_ref, solution_ref, residual_ref):
    for plane in range(code_ref.shape[0]):
        scales = jnp.exp2(widen(code_ref[plane, 2 * SHARE * COLS :, :]) - 15.0)
        for part, ref in enumerate((solution_ref, residual_ref)):
            scale = scales[part * COLS : (part + 1) * COLS]
            for inner in range(0, SHARE, 2):
                row = (part * SHARE + inner) * COLS
                values = widen(code_ref[plane, row : row + 2 * COLS, :])
                columns = slice(plane * COLS, (plane + 1) * COLS)
                ref[inner, columns, :] = values[:COLS] * scale
                ref[inner + 1, columns, :] = values[COLS:] * scale


WHOLE = pl.BlockSpec(memory_space=pltpu.VMEM)
SCALARS = pl.BlockSpec(memory_space=pltpu.SMEM)
PARAMS = pltpu.CompilerParams(vmem_limit_bytes=VMEM_LIMIT)


def start_call(shaped, residual):
    blocks = shaped.shape[0]
    return pl.pallas_call(
        start_kernel,
        out_shape=jax.ShapeDtypeStruct((blocks * COLS + EXTRA, LANES), I16),
        in_specs=[WHOLE, WHOLE],
        out_specs=WHOLE,
        compiler_params=PARAMS,
        name="start",
    )(shaped, residual)


def factor_call(first, last, near, me, codes, shaped, precision, tiles, state):
    peers = codes.shape[0]
    blocks = shaped.shape[0]
    field = (peers * blocks, 2 * COLS, LANES)

    arguments = (near, me, codes, shaped, precision, tiles, *state)
    outs = [
        (codes.shape, I16),
        (shaped.shape, F32),
        (shaped.shape, F32),
        ((COLS, LANES), F32),
    ]
    scratch = [
        pltpu.VMEM((peers * blocks, COLS, LANES), F32),
        pltpu.VMEM((COLS, LANES), F32),
        pltpu.VMEM((BUFFERS,) + tiles.shape[1:], BF16),
        pltpu.SemaphoreType.DMA((BUFFERS,)),
    ]
    if last:
        scratch = [pltpu.VMEM(field, BF16)] + scratch
    else:
        outs.append((field, BF16))
    return pl.pallas_call(
        lambda *refs: factor_kernel(first, last, peers, *refs),
        out_shape=[jax.ShapeDtypeStruct(*out) for out in outs],
        in_specs=[SCALARS] * 2
        + [WHOLE] * 3
        + [pl.BlockSpec(memory_space=pl.ANY)]
        + [WHOLE] * (len(arguments) - 6),
        out_specs=[WHOLE] * len(outs),
        scratch_shapes=scratch,
        compiler_params=pltpu.CompilerParams(vmem_limit_bytes=STREAM_LIMIT),
        name="factor",
    )(*arguments)


def update_call(last, me, codes, own, residual, answer, direction, gamma, precond):
    shape = jax.ShapeDtypeStruct(own.shape, F32)
    arguments = [me, codes, own, residual, answer, direction, gamma]
    if last:
        rows = 2 * SHARE * COLS + 2 * COLS
        outs = [jax.ShapeDtypeStruct((own.shape[0] // SHARE, rows, LANES), I16)]
        scratch = [pltpu.VMEM(own.shape, F32)] * 3
    else:
        outs = [shape, shape, shape, jax.ShapeDtypeStruct(codes.shape[1:], I16)]
        scratch = [pltpu.VMEM(own.shape, F32)]
        arguments.append(precond)
    in_specs = [SCALARS] + [WHOLE] * (len(arguments) - 1)
    return pl.pallas_call(
        lambda *refs: update_kernel(last, codes.shape[0], *refs),
        out_shape=outs,
        in_specs=in_specs,
        out_specs=[WHOLE] * len(outs),
        scratch_shapes=scratch,
        compiler_params=PARAMS,
        name="update",
    )(*arguments)


def finish_call(codes):
    shape = jax.ShapeDtypeStruct((SHARE, codes.shape[0] * COLS, LANES), F32)
    return pl.pallas_call(
        finish_kernel,
        out_shape=[shape, shape],
        in_specs=[WHOLE],
        out_specs=[WHOLE, WHOLE],
        compiler_params=PARAMS,
        name="finish",
    )(codes)


def local(right_side, diag_tiles, cond_tiles, neighbour_blocks, precision_diag, precond_tiles):
    depth, wide, high = (lax.axis_size(name) for name in ("z", "x", "y"))
    peers = wide * high
    here = right_side.shape[0]
    blocks = depth * here
    core = lax.axis_index("c")
    me = (lax.axis_index("x") * high + lax.axis_index("y")).astype(I32).reshape(1)
    half = here // 2

    own_diag = jnp.where(core == 0, diag_tiles[:half], diag_tiles[half:])
    mine = jnp.concatenate([cond_tiles.reshape(-1, LANES, LANES), own_diag], axis=0)
    tiles = lax.all_gather(mine, ("z", "c"), axis=0, tiled=False)
    tiles = tiles.reshape((depth, 2) + mine.shape)
    own_precond = lax.dynamic_slice_in_dim(precond_tiles, core * half, half, 0)

    wide_precond = precond_tiles.astype(F32)
    shaped = jnp.einsum("lts,lcs->lct", wide_precond, right_side, precision=lax.Precision.HIGHEST)
    near = jnp.pad(neighbour_blocks.astype(F32), ((0, 0), (0, LANES - neighbour_blocks.shape[1])))
    facts = jnp.concatenate([precision_diag, near], axis=0)
    facts = jnp.broadcast_to(facts[None], (depth,) + facts.shape)

    def by_column(values):
        values = values.reshape(here, depth, COLS, LANES).transpose(1, 0, 2, 3)
        return values.reshape(depth, here * COLS, LANES)

    sent = jnp.concatenate([by_column(right_side), by_column(shaped), facts], axis=1)
    came = lax.all_to_all(sent, "z", split_axis=0, concat_axis=0, tiled=True)
    rows = here * COLS
    residual = came[:, :rows].reshape(blocks, COLS, LANES)
    shaped = came[:, rows : 2 * rows].reshape(blocks, COLS, LANES)
    precision = came[:, 2 * rows : 2 * rows + here].reshape(blocks, LANES)
    near = came[:, 2 * rows + here :, : neighbour_blocks.shape[1]].astype(I32).reshape(-1)
    plane = near // (peers * here)
    near = (near // here) % peers * blocks + plane * here + near % here

    answer = jnp.zeros_like(residual)
    codes = start_call(shaped, residual)
    state = ()
    for iteration in range(ITERS):
        last = iteration + 1 == ITERS
        arrived = lax.all_gather(codes, ("x", "y"), axis=0, tiled=False)
        if iteration == 0:
            arrived, near, precision, tiles, own_precond = lax.optimization_barrier(
                (arrived, near, precision, tiles, own_precond)
            )
            precond = lax.all_gather(own_precond, ("z", "c"), axis=0, tiled=True)
        leaving, own, direction, gamma, *field = factor_call(
            iteration == 0, last, near, me, arrived, shaped, precision, tiles, state
        )
        terms = lax.all_to_all(leaving, ("x", "y"), split_axis=0, concat_axis=0, tiled=True)
        results = update_call(
            last, me, terms, own, residual, answer, direction, gamma, precond
        )
        if not last:
            residual, answer, shaped, codes = results
            state = (field[0], direction, gamma)

    codes = lax.all_to_all(results[0], "z", split_axis=0, concat_axis=0, tiled=True)
    answer, residual = finish_call(codes)
    return answer, residual


def solution(mesh, dims=DIMS):
    grid = Mesh(np.asarray(mesh.devices).reshape(dims + (2,)), ("z", "x", "y", "c"))
    blk = ("z", "x", "y")
    return jax.shard_map(
        local,
        mesh=grid,
        in_specs=(P(blk, "c", None), P(blk), P(blk, "c"), P(blk), P(blk), P(blk)),
        out_specs=(P(blk, "c", None), P(blk, "c", None)),
        check_vma=False,
    )
```

```python
import jax
import jax.numpy as jnp
import numpy as np
from jax import lax
from jax.experimental import pallas as pl
from jax.experimental.pallas import tpu as pltpu
from jax.sharding import Mesh, PartitionSpec as P

ITERS = 3
DIMS = (8, 4, 4)
LANES = 128
COLS = 8
SHARE = 8
GROUPS = 3
EXTRA = (GROUPS + 1) * COLS
BUFFERS = 8
LOW_EXP = -100.0
F32, BF16, I16, I32 = jnp.float32, jnp.bfloat16, jnp.int16, jnp.int32
VMEM_LIMIT = 12 * 1024 * 1024
STREAM_LIMIT = 36 * 1024 * 1024


def spread(column):
    return jnp.broadcast_to(column, (column.shape[0], LANES))


def split_rows(values):
    lead = values.astype(BF16).astype(F32)
    return jnp.concatenate([lead, values - lead], axis=0).astype(BF16)


def join_rows(values):
    return values[:COLS] + values[COLS:]


def group_ranges(blocks):
    pairs = blocks // 2
    cuts = [2 * (pairs * part // GROUPS) for part in range(GROUPS + 1)]
    return list(zip(cuts[:-1], cuts[1:]))


def exponents(tops):
    exps = jnp.floor(jnp.log2(jnp.maximum(tops, 1e-35) * 1.0025)) + 1.0
    return jnp.clip(exps, LOW_EXP, 126.0)


def encode(read, blocks, partial, write):
    tail = []
    for low, high in group_ranges(blocks):
        tops = jnp.abs(read(low))
        for block in range(low + 1, high):
            tops = jnp.maximum(tops, jnp.abs(read(block)))
        exps = exponents(tops)
        tail.append(exps)
        scale = jnp.exp2(15.0 - exps)
        for block in range(low, high, 2):
            pair = jnp.concatenate([read(block) * scale, read(block + 1) * scale], axis=0)
            write(block * COLS, jnp.round(pair).astype(I32).astype(I16))
    total = spread(jnp.sum(partial, axis=1, keepdims=True))
    exps = exponents(jnp.abs(total))
    scaled = total * (jnp.exp2(15.0 - exps) * 0.5)
    first = jnp.round(scaled)
    second = jnp.round((scaled - first) * 32768.0)
    lane = lax.broadcasted_iota(I32, (COLS, LANES), 1)
    tail.append(jnp.where(lane == 0, exps, jnp.where(lane == 1, first, second)))
    for part in range(0, GROUPS + 1, 2):
        rows = jnp.concatenate(tail[part : part + 2], axis=0)
        write((blocks + part) * COLS, rows.astype(I32).astype(I16))


def widen(rows):
    return rows.astype(I32).astype(F32)


def decode_tail(rows):
    rows = widen(rows)
    scales = [jnp.exp2(rows[part * COLS : (part + 1) * COLS] - 15.0) for part in range(GROUPS)]
    tail = rows[GROUPS * COLS :]
    whole = tail[:, 1:2] + tail[:, 2:3] * (1.0 / 32768.0)
    total = spread(whole) * (jnp.exp2(spread(tail[:, 0:1]) - 15.0) * 2.0)
    return scales, total


def decode_blocks(read, scales, blocks, take):
    for scale, (low, high) in zip(scales, group_ranges(blocks)):
        for block in range(low, high, 2):
            values = widen(read(block * COLS))
            take(block, values[:COLS] * scale)
            take(block + 1, values[COLS:] * scale)


def start_kernel(shaped_ref, residual_ref, code_ref):
    blocks = shaped_ref.shape[0]
    partial = jnp.zeros((COLS, LANES), F32)
    for block in range(blocks):
        partial = partial + shaped_ref[block] * residual_ref[block]

    def write(row, value):
        code_ref[row : row + 2 * COLS, :] = value

    encode(lambda block: shaped_ref[block], blocks, partial, write)


def factor_kernel(first, last, peers, *refs):
    refs = list(refs)
    near_ref, me_ref, code_ref, shaped_ref, precision_ref, tiles_ref = refs[:6]
    refs = refs[6:]
    if not first:
        old_field_ref, old_direction_ref, old_gamma_ref = refs[:3]
        refs = refs[3:]
    out_ref, own_ref, direction_ref, gamma_ref = refs[:4]
    field_ref, running_ref, partial_ref, held_ref, semaphores = refs[4:]
    blocks = shaped_ref.shape[0]
    step_blocks = SHARE
    steps = blocks // step_blocks
    half = step_blocks // 2
    slots = 4
    buffers = held_ref.shape[0]

    def fetch(step):
        buffer = lax.rem(step, buffers)
        return pltpu.make_async_copy(tiles_ref.at[step], held_ref.at[buffer], semaphores.at[buffer])

    for step in range(min(buffers, steps)):
        fetch(step).start()

    def prologue():
        gamma = jnp.zeros((COLS, LANES), F32)
        for peer in range(peers):
            gamma = gamma + decode_tail(code_ref[peer, blocks * COLS :, :])[1]
        gamma_ref[...] = gamma
        if not first:
            beta = gamma / old_gamma_ref[...]

        def take(peer, carry):
            scales, unused = decode_tail(code_ref[peer, blocks * COLS :, :])

            def keep(block, values):
                place = peer * blocks + block
                if not first:
                    values = values + beta * join_rows(old_field_ref[place].astype(F32))
                field_ref[place] = split_rows(values)
                running_ref[place] = jnp.zeros((COLS, LANES), F32)

            def read(row):
                return code_ref[peer, row : row + 2 * COLS, :]

            decode_blocks(read, scales, blocks, keep)
            return carry

        lax.fori_loop(0, peers, take, 0)
        for block in range(blocks):
            values = shaped_ref[block]
            if not first:
                values = values + beta * old_direction_ref[block]
            direction_ref[block] = values
        partial_ref[...] = jnp.zeros_like(partial_ref)

    def work(step, at):
        def tile_row(inner):
            parts = [
                held_ref[at, core, inner * slots + slot]
                for core in range(2)
                for slot in range(slots)
            ]
            parts.append(held_ref[at, inner // half, slots * step_blocks + inner % half])
            return jnp.concatenate(parts, axis=1)

        partial = partial_ref[...]
        kept = []
        for inner in range(step_blocks):
            block = step * step_blocks + inner
            places = [near_ref[block * 2 * slots + k] for k in range(2 * slots)]
            left = [field_ref[place] for place in places] + [split_rows(direction_ref[block])]
            summed = join_rows(
                lax.dot_general(
                    jnp.concatenate(left, axis=1),
                    tile_row(inner),
                    (((1,), (1,)), ((), ())),
                    preferred_element_type=F32,
                )
            )
            weighted = precision_ref[pl.ds(block, 1), :] * summed
            partial = partial + weighted * summed
            kept.append((block, places, split_rows(weighted)))
        partial_ref[...] = partial
        for inner, (block, places, weighted) in enumerate(kept):
            pieces = join_rows(
                jnp.dot(weighted, tile_row(inner), preferred_element_type=F32)
            )
            own_ref[block] = pieces[:, 2 * slots * LANES :]
            for k, place in enumerate(places):
                running_ref[place] = running_ref[place] + pieces[:, k * LANES : (k + 1) * LANES]

    def epilogue():
        me = me_ref[0]
        for block in range(blocks):
            own_ref[block] = own_ref[block] + running_ref[me * blocks + block]

        def give(peer, carry):
            def write(row, value):
                out_ref[peer, row : row + 2 * COLS, :] = value

            encode(lambda block: running_ref[peer * blocks + block], blocks, partial_ref[...], write)
            return carry

        lax.fori_loop(0, peers, give, 0)

    def loop(step, carry):
        fetch(step).wait()
        work(step, lax.rem(step, buffers))

        @pl.when(step + buffers < steps)
        def refill():
            fetch(step + buffers).start()

        return carry

    prologue()
    lax.fori_loop(0, steps, loop, 0)
    epilogue()


def update_kernel(last, peers, *refs):
    refs = list(refs)
    me_ref, code_ref, own_ref, residual_ref, solution_ref, direction_ref, gamma_ref = refs[:7]
    refs = refs[7:]
    if last:
        out_ref, new_residual_ref, new_solution_ref, image_ref = refs
    else:
        precond_ref, new_residual_ref, new_solution_ref, shaped_ref, out_ref, image_ref = refs
    blocks = own_ref.shape[0]
    me = me_ref[0]
    for block in range(blocks):
        image_ref[block] = own_ref[block]

    def take(peer, bottom):
        scales, total = decode_tail(code_ref[peer, blocks * COLS :, :])
        scales = [jnp.where(peer == me, 0.0, scale) for scale in scales]

        def read(row):
            return code_ref[peer, row : row + 2 * COLS, :]

        def add(block, values):
            image_ref[block] = image_ref[block] + values

        decode_blocks(read, scales, blocks, add)
        return bottom + total

    bottom = lax.fori_loop(0, peers, take, jnp.zeros((COLS, LANES), F32))
    alpha = gamma_ref[...] / bottom
    partial = jnp.zeros((COLS, LANES), F32)
    for block in range(blocks):
        new_solution_ref[block] = solution_ref[block] + alpha * direction_ref[block]
        residual = residual_ref[block] - alpha * image_ref[block]
        new_residual_ref[block] = residual
        if not last:
            shaped = join_rows(
                jnp.dot(split_rows(residual), precond_ref[block], preferred_element_type=F32)
            )
            shaped_ref[block] = shaped
            partial = partial + residual * shaped
    if not last:

        def write(row, value):
            out_ref[row : row + 2 * COLS, :] = value

        encode(lambda block: shaped_ref[block], blocks, partial, write)
    else:
        for plane in range(blocks // SHARE):
            for part, ref in enumerate((new_solution_ref, new_residual_ref)):
                first = plane * SHARE
                tops = jnp.abs(ref[first])
                for inner in range(1, SHARE):
                    tops = jnp.maximum(tops, jnp.abs(ref[first + inner]))
                exps = exponents(tops)
                scale = jnp.exp2(15.0 - exps)
                for inner in range(0, SHARE, 2):
                    pair = jnp.concatenate(
                        [ref[first + inner] * scale, ref[first + inner + 1] * scale], axis=0
                    )
                    row = (part * SHARE + inner) * COLS
                    out_ref[plane, row : row + 2 * COLS, :] = jnp.round(pair).astype(I32).astype(I16)
                kept = exps if part == 0 else jnp.concatenate([kept, exps], axis=0)
            out_ref[plane, 2 * SHARE * COLS :, :] = kept.astype(I32).astype(I16)


def finish_kernel(code_ref, solution_ref, residual_ref):
    for plane in range(code_ref.shape[0]):
        scales = jnp.exp2(widen(code_ref[plane, 2 * SHARE * COLS :, :]) - 15.0)
        for part, ref in enumerate((solution_ref, residual_ref)):
            scale = scales[part * COLS : (part + 1) * COLS]
            for inner in range(0, SHARE, 2):
                row = (part * SHARE + inner) * COLS
                values = widen(code_ref[plane, row : row + 2 * COLS, :])
                columns = slice(plane * COLS, (plane + 1) * COLS)
                ref[inner, columns, :] = values[:COLS] * scale
                ref[inner + 1, columns, :] = values[COLS:] * scale


WHOLE = pl.BlockSpec(memory_space=pltpu.VMEM)
SCALARS = pl.BlockSpec(memory_space=pltpu.SMEM)
PARAMS = pltpu.CompilerParams(vmem_limit_bytes=VMEM_LIMIT)


def start_call(shaped, residual):
    blocks = shaped.shape[0]
    return pl.pallas_call(
        start_kernel,
        out_shape=jax.ShapeDtypeStruct((blocks * COLS + EXTRA, LANES), I16),
        in_specs=[WHOLE, WHOLE],
        out_specs=WHOLE,
        compiler_params=PARAMS,
        name="start",
    )(shaped, residual)


def factor_call(first, last, near, me, codes, shaped, precision, tiles, state):
    peers = codes.shape[0]
    blocks = shaped.shape[0]
    field = (peers * blocks, 2 * COLS, LANES)

    arguments = (near, me, codes, shaped, precision, tiles, *state)
    outs = [
        (codes.shape, I16),
        (shaped.shape, F32),
        (shaped.shape, F32),
        ((COLS, LANES), F32),
    ]
    scratch = [
        pltpu.VMEM((peers * blocks, COLS, LANES), F32),
        pltpu.VMEM((COLS, LANES), F32),
        pltpu.VMEM((BUFFERS,) + tiles.shape[1:], BF16),
        pltpu.SemaphoreType.DMA((BUFFERS,)),
    ]
    if last:
        scratch = [pltpu.VMEM(field, BF16)] + scratch
    else:
        outs.append((field, BF16))
    return pl.pallas_call(
        lambda *refs: factor_kernel(first, last, peers, *refs),
        out_shape=[jax.ShapeDtypeStruct(*out) for out in outs],
        in_specs=[SCALARS] * 2
        + [WHOLE] * 3
        + [pl.BlockSpec(memory_space=pl.ANY)]
        + [WHOLE] * (len(arguments) - 6),
        out_specs=[WHOLE] * len(outs),
        scratch_shapes=scratch,
        compiler_params=pltpu.CompilerParams(vmem_limit_bytes=STREAM_LIMIT),
        name="factor",
    )(*arguments)


def update_call(last, me, codes, own, residual, answer, direction, gamma, precond):
    shape = jax.ShapeDtypeStruct(own.shape, F32)
    arguments = [me, codes, own, residual, answer, direction, gamma]
    if last:
        rows = 2 * SHARE * COLS + 2 * COLS
        outs = [jax.ShapeDtypeStruct((own.shape[0] // SHARE, rows, LANES), I16)]
        scratch = [pltpu.VMEM(own.shape, F32)] * 3
    else:
        outs = [shape, shape, shape, jax.ShapeDtypeStruct(codes.shape[1:], I16)]
        scratch = [pltpu.VMEM(own.shape, F32)]
        arguments.append(precond)
    in_specs = [SCALARS] + [WHOLE] * (len(arguments) - 1)
    return pl.pallas_call(
        lambda *refs: update_kernel(last, codes.shape[0], *refs),
        out_shape=outs,
        in_specs=in_specs,
        out_specs=[WHOLE] * len(outs),
        scratch_shapes=scratch,
        compiler_params=PARAMS,
        name="update",
    )(*arguments)


def finish_call(codes):
    shape = jax.ShapeDtypeStruct((SHARE, codes.shape[0] * COLS, LANES), F32)
    return pl.pallas_call(
        finish_kernel,
        out_shape=[shape, shape],
        in_specs=[WHOLE],
        out_specs=[WHOLE, WHOLE],
        compiler_params=PARAMS,
        name="finish",
    )(codes)


def local(right_side, diag_tiles, cond_tiles, neighbour_blocks, precision_diag, precond_tiles):
    depth, wide, high = (lax.axis_size(name) for name in ("z", "x", "y"))
    peers = wide * high
    here = right_side.shape[0]
    blocks = depth * here
    core = lax.axis_index("c")
    me = (lax.axis_index("x") * high + lax.axis_index("y")).astype(I32).reshape(1)
    half = here // 2

    own_diag = jnp.where(core == 0, diag_tiles[:half], diag_tiles[half:])
    mine = jnp.concatenate([cond_tiles.reshape(-1, LANES, LANES), own_diag], axis=0)
    tiles = lax.all_gather(mine, ("z", "c"), axis=0, tiled=False)
    tiles = tiles.reshape((depth, 2) + mine.shape)
    own_precond = lax.dynamic_slice_in_dim(precond_tiles, core * half, half, 0)

    wide_precond = precond_tiles.astype(F32)
    shaped = jnp.einsum("lts,lcs->lct", wide_precond, right_side, precision=lax.Precision.HIGHEST)
    near = jnp.pad(neighbour_blocks.astype(F32), ((0, 0), (0, LANES - neighbour_blocks.shape[1])))
    facts = jnp.concatenate([precision_diag, near], axis=0)
    facts = jnp.broadcast_to(facts[None], (depth,) + facts.shape)

    def by_column(values):
        values = values.reshape(here, depth, COLS, LANES).transpose(1, 0, 2, 3)
        return values.reshape(depth, here * COLS, LANES)

    sent = jnp.concatenate([by_column(right_side), by_column(shaped), facts], axis=1)
    came = lax.all_to_all(sent, "z", split_axis=0, concat_axis=0, tiled=True)
    rows = here * COLS
    residual = came[:, :rows].reshape(blocks, COLS, LANES)
    shaped = came[:, rows : 2 * rows].reshape(blocks, COLS, LANES)
    precision = came[:, 2 * rows : 2 * rows + here].reshape(blocks, LANES)
    near = came[:, 2 * rows + here :, : neighbour_blocks.shape[1]].astype(I32).reshape(-1)
    plane = near // (peers * here)
    near = (near // here) % peers * blocks + plane * here + near % here

    answer = jnp.zeros_like(residual)
    codes = start_call(shaped, residual)
    state = ()
    for iteration in range(ITERS):
        last = iteration + 1 == ITERS
        arrived = lax.all_gather(codes, ("x", "y"), axis=0, tiled=False)
        if iteration == 0:
            arrived, near, precision, tiles, own_precond = lax.optimization_barrier(
                (arrived, near, precision, tiles, own_precond)
            )
            precond = lax.all_gather(own_precond, ("z", "c"), axis=0, tiled=True)
        leaving, own, direction, gamma, *field = factor_call(
            iteration == 0, last, near, me, arrived, shaped, precision, tiles, state
        )
        terms = lax.all_to_all(leaving, ("x", "y"), split_axis=0, concat_axis=0, tiled=True)
        results = update_call(
            last, me, terms, own, residual, answer, direction, gamma, precond
        )
        if not last:
            residual, answer, shaped, codes = results
            state = (field[0], direction, gamma)

    codes = lax.all_to_all(results[0], "z", split_axis=0, concat_axis=0, tiled=True)
    answer, residual = finish_call(codes)
    return answer, residual


def solution(mesh, dims=DIMS):
    grid = Mesh(np.asarray(mesh.devices).reshape(dims + (2,)), ("z", "x", "y", "c"))
    blk = ("z", "x", "y")
    return jax.shard_map(
        local,
        mesh=grid,
        in_specs=(P(blk, "c", None), P(blk), P(blk, "c"), P(blk), P(blk), P(blk)),
        out_specs=(P(blk, "c", None), P(blk, "c", None)),
        check_vma=False,
    )
```

```python
import jax
import jax.numpy as jnp
import numpy as np
from jax import lax
from jax.experimental import pallas as pl
from jax.experimental.pallas import tpu as pltpu
from jax.sharding import Mesh, PartitionSpec as P

ITERS = 3
DIMS = (8, 4, 4)
LANES = 128
COLS = 8
SHARE = 8
GROUPS = 1
EXTRA = (GROUPS + 1) * COLS
BUFFERS = 8
LOW_EXP = -100.0
F32, BF16, I16, I32 = jnp.float32, jnp.bfloat16, jnp.int16, jnp.int32
VMEM_LIMIT = 12 * 1024 * 1024
STREAM_LIMIT = 36 * 1024 * 1024


def spread(column):
    return jnp.broadcast_to(column, (column.shape[0], LANES))


def split_rows(values):
    lead = values.astype(BF16).astype(F32)
    return jnp.concatenate([lead, values - lead], axis=0).astype(BF16)


def join_rows(values):
    return values[:COLS] + values[COLS:]


def group_ranges(blocks):
    pairs = blocks // 2
    cuts = [2 * (pairs * part // GROUPS) for part in range(GROUPS + 1)]
    return list(zip(cuts[:-1], cuts[1:]))


def exponents(tops):
    exps = jnp.floor(jnp.log2(jnp.maximum(tops, 1e-35) * 1.0025)) + 1.0
    return jnp.clip(exps, LOW_EXP, 126.0)


def encode(read, blocks, partial, write):
    tail = []
    for low, high in group_ranges(blocks):
        tops = jnp.abs(read(low))
        for block in range(low + 1, high):
            tops = jnp.maximum(tops, jnp.abs(read(block)))
        exps = exponents(tops)
        tail.append(exps)
        scale = jnp.exp2(15.0 - exps)
        for block in range(low, high, 2):
            pair = jnp.concatenate([read(block) * scale, read(block + 1) * scale], axis=0)
            write(block * COLS, jnp.round(pair).astype(I32).astype(I16))
    total = spread(jnp.sum(partial, axis=1, keepdims=True))
    exps = exponents(jnp.abs(total))
    scaled = total * (jnp.exp2(15.0 - exps) * 0.5)
    first = jnp.round(scaled)
    second = jnp.round((scaled - first) * 32768.0)
    lane = lax.broadcasted_iota(I32, (COLS, LANES), 1)
    tail.append(jnp.where(lane == 0, exps, jnp.where(lane == 1, first, second)))
    for part in range(0, GROUPS + 1, 2):
        rows = jnp.concatenate(tail[part : part + 2], axis=0)
        write((blocks + part) * COLS, rows.astype(I32).astype(I16))


def widen(rows):
    return rows.astype(I32).astype(F32)


def decode_tail(rows):
    rows = widen(rows)
    scales = [jnp.exp2(rows[part * COLS : (part + 1) * COLS] - 15.0) for part in range(GROUPS)]
    tail = rows[GROUPS * COLS :]
    whole = tail[:, 1:2] + tail[:, 2:3] * (1.0 / 32768.0)
    total = spread(whole) * (jnp.exp2(spread(tail[:, 0:1]) - 15.0) * 2.0)
    return scales, total


def decode_blocks(read, scales, blocks, take):
    for scale, (low, high) in zip(scales, group_ranges(blocks)):
        for block in range(low, high, 2):
            values = widen(read(block * COLS))
            take(block, values[:COLS] * scale)
            take(block + 1, values[COLS:] * scale)


def start_kernel(shaped_ref, residual_ref, code_ref):
    blocks = shaped_ref.shape[0]
    partial = jnp.zeros((COLS, LANES), F32)
    for block in range(blocks):
        partial = partial + shaped_ref[block] * residual_ref[block]

    def write(row, value):
        code_ref[row : row + 2 * COLS, :] = value

    encode(lambda block: shaped_ref[block], blocks, partial, write)


def factor_kernel(first, last, peers, *refs):
    refs = list(refs)
    near_ref, me_ref, code_ref, shaped_ref, precision_ref, tiles_ref = refs[:6]
    refs = refs[6:]
    if not first:
        old_field_ref, old_direction_ref, old_gamma_ref = refs[:3]
        refs = refs[3:]
    out_ref, own_ref, direction_ref, gamma_ref = refs[:4]
    field_ref, running_ref, partial_ref, held_ref, semaphores = refs[4:]
    blocks = shaped_ref.shape[0]
    step_blocks = SHARE
    steps = blocks // step_blocks
    half = step_blocks // 2
    slots = 4
    buffers = held_ref.shape[0]

    def fetch(step):
        buffer = lax.rem(step, buffers)
        return pltpu.make_async_copy(tiles_ref.at[step], held_ref.at[buffer], semaphores.at[buffer])

    for step in range(min(buffers, steps)):
        fetch(step).start()

    def prologue():
        gamma = jnp.zeros((COLS, LANES), F32)
        for peer in range(peers):
            gamma = gamma + decode_tail(code_ref[peer, blocks * COLS :, :])[1]
        gamma_ref[...] = gamma
        if not first:
            beta = gamma / old_gamma_ref[...]

        def take(peer, carry):
            scales, unused = decode_tail(code_ref[peer, blocks * COLS :, :])

            def keep(block, values):
                place = peer * blocks + block
                if not first:
                    values = values + beta * join_rows(old_field_ref[place].astype(F32))
                field_ref[place] = split_rows(values)
                running_ref[place] = jnp.zeros((COLS, LANES), F32)

            def read(row):
                return code_ref[peer, row : row + 2 * COLS, :]

            decode_blocks(read, scales, blocks, keep)
            return carry

        lax.fori_loop(0, peers, take, 0)
        for block in range(blocks):
            values = shaped_ref[block]
            if not first:
                values = values + beta * old_direction_ref[block]
            direction_ref[block] = values
        partial_ref[...] = jnp.zeros_like(partial_ref)

    def work(step, at):
        def tile_row(inner):
            parts = [
                held_ref[at, core, inner * slots + slot]
                for core in range(2)
                for slot in range(slots)
            ]
            parts.append(held_ref[at, inner // half, slots * step_blocks + inner % half])
            return jnp.concatenate(parts, axis=1)

        partial = partial_ref[...]
        kept = []
        for inner in range(step_blocks):
            block = step * step_blocks + inner
            places = [near_ref[block * 2 * slots + k] for k in range(2 * slots)]
            left = [field_ref[place] for place in places] + [split_rows(direction_ref[block])]
            summed = join_rows(
                lax.dot_general(
                    jnp.concatenate(left, axis=1),
                    tile_row(inner),
                    (((1,), (1,)), ((), ())),
                    preferred_element_type=F32,
                )
            )
            weighted = precision_ref[pl.ds(block, 1), :] * summed
            partial = partial + weighted * summed
            kept.append((block, places, split_rows(weighted)))
        partial_ref[...] = partial
        for inner, (block, places, weighted) in enumerate(kept):
            pieces = join_rows(
                jnp.dot(weighted, tile_row(inner), preferred_element_type=F32)
            )
            own_ref[block] = pieces[:, 2 * slots * LANES :]
            for k, place in enumerate(places):
                running_ref[place] = running_ref[place] + pieces[:, k * LANES : (k + 1) * LANES]

    def epilogue():
        me = me_ref[0]
        for block in range(blocks):
            own_ref[block] = own_ref[block] + running_ref[me * blocks + block]

        def give(peer, carry):
            def write(row, value):
                out_ref[peer, row : row + 2 * COLS, :] = value

            encode(lambda block: running_ref[peer * blocks + block], blocks, partial_ref[...], write)
            return carry

        lax.fori_loop(0, peers, give, 0)

    def loop(step, carry):
        fetch(step).wait()
        work(step, lax.rem(step, buffers))

        @pl.when(step + buffers < steps)
        def refill():
            fetch(step + buffers).start()

        return carry

    prologue()
    lax.fori_loop(0, steps, loop, 0)
    epilogue()


def update_kernel(last, peers, *refs):
    refs = list(refs)
    me_ref, code_ref, own_ref, residual_ref, solution_ref, direction_ref, gamma_ref = refs[:7]
    refs = refs[7:]
    if last:
        out_ref, new_residual_ref, new_solution_ref, image_ref = refs
    else:
        precond_ref, new_residual_ref, new_solution_ref, shaped_ref, out_ref, image_ref = refs
    blocks = own_ref.shape[0]
    me = me_ref[0]
    for block in range(blocks):
        image_ref[block] = own_ref[block]

    def take(peer, bottom):
        scales, total = decode_tail(code_ref[peer, blocks * COLS :, :])
        scales = [jnp.where(peer == me, 0.0, scale) for scale in scales]

        def read(row):
            return code_ref[peer, row : row + 2 * COLS, :]

        def add(block, values):
            image_ref[block] = image_ref[block] + values

        decode_blocks(read, scales, blocks, add)
        return bottom + total

    bottom = lax.fori_loop(0, peers, take, jnp.zeros((COLS, LANES), F32))
    alpha = gamma_ref[...] / bottom
    partial = jnp.zeros((COLS, LANES), F32)
    for block in range(blocks):
        new_solution_ref[block] = solution_ref[block] + alpha * direction_ref[block]
        residual = residual_ref[block] - alpha * image_ref[block]
        new_residual_ref[block] = residual
        if not last:
            shaped = join_rows(
                jnp.dot(split_rows(residual), precond_ref[block], preferred_element_type=F32)
            )
            shaped_ref[block] = shaped
            partial = partial + residual * shaped
    if not last:

        def write(row, value):
            out_ref[row : row + 2 * COLS, :] = value

        encode(lambda block: shaped_ref[block], blocks, partial, write)
    else:
        for plane in range(blocks // SHARE):
            for part, ref in enumerate((new_solution_ref, new_residual_ref)):
                first = plane * SHARE
                tops = jnp.abs(ref[first])
                for inner in range(1, SHARE):
                    tops = jnp.maximum(tops, jnp.abs(ref[first + inner]))
                exps = exponents(tops)
                scale = jnp.exp2(15.0 - exps)
                for inner in range(0, SHARE, 2):
                    pair = jnp.concatenate(
                        [ref[first + inner] * scale, ref[first + inner + 1] * scale], axis=0
                    )
                    row = (part * SHARE + inner) * COLS
                    out_ref[plane, row : row + 2 * COLS, :] = jnp.round(pair).astype(I32).astype(I16)
                kept = exps if part == 0 else jnp.concatenate([kept, exps], axis=0)
            out_ref[plane, 2 * SHARE * COLS :, :] = kept.astype(I32).astype(I16)


def finish_kernel(code_ref, solution_ref, residual_ref):
    for plane in range(code_ref.shape[0]):
        scales = jnp.exp2(widen(code_ref[plane, 2 * SHARE * COLS :, :]) - 15.0)
        for part, ref in enumerate((solution_ref, residual_ref)):
            scale = scales[part * COLS : (part + 1) * COLS]
            for inner in range(0, SHARE, 2):
                row = (part * SHARE + inner) * COLS
                values = widen(code_ref[plane, row : row + 2 * COLS, :])
                columns = slice(plane * COLS, (plane + 1) * COLS)
                ref[inner, columns, :] = values[:COLS] * scale
                ref[inner + 1, columns, :] = values[COLS:] * scale


WHOLE = pl.BlockSpec(memory_space=pltpu.VMEM)
SCALARS = pl.BlockSpec(memory_space=pltpu.SMEM)
PARAMS = pltpu.CompilerParams(vmem_limit_bytes=VMEM_LIMIT)


def start_call(shaped, residual):
    blocks = shaped.shape[0]
    return pl.pallas_call(
        start_kernel,
        out_shape=jax.ShapeDtypeStruct((blocks * COLS + EXTRA, LANES), I16),
        in_specs=[WHOLE, WHOLE],
        out_specs=WHOLE,
        compiler_params=PARAMS,
        name="start",
    )(shaped, residual)


def factor_call(first, last, near, me, codes, shaped, precision, tiles, state):
    peers = codes.shape[0]
    blocks = shaped.shape[0]
    field = (peers * blocks, 2 * COLS, LANES)

    arguments = (near, me, codes, shaped, precision, tiles, *state)
    outs = [
        (codes.shape, I16),
        (shaped.shape, F32),
        (shaped.shape, F32),
        ((COLS, LANES), F32),
    ]
    scratch = [
        pltpu.VMEM((peers * blocks, COLS, LANES), F32),
        pltpu.VMEM((COLS, LANES), F32),
        pltpu.VMEM((BUFFERS,) + tiles.shape[1:], BF16),
        pltpu.SemaphoreType.DMA((BUFFERS,)),
    ]
    if last:
        scratch = [pltpu.VMEM(field, BF16)] + scratch
    else:
        outs.append((field, BF16))
    return pl.pallas_call(
        lambda *refs: factor_kernel(first, last, peers, *refs),
        out_shape=[jax.ShapeDtypeStruct(*out) for out in outs],
        in_specs=[SCALARS] * 2
        + [WHOLE] * 3
        + [pl.BlockSpec(memory_space=pl.ANY)]
        + [WHOLE] * (len(arguments) - 6),
        out_specs=[WHOLE] * len(outs),
        scratch_shapes=scratch,
        compiler_params=pltpu.CompilerParams(vmem_limit_bytes=STREAM_LIMIT),
        name="factor",
    )(*arguments)


def update_call(last, me, codes, own, residual, answer, direction, gamma, precond):
    shape = jax.ShapeDtypeStruct(own.shape, F32)
    arguments = [me, codes, own, residual, answer, direction, gamma]
    if last:
        rows = 2 * SHARE * COLS + 2 * COLS
        outs = [jax.ShapeDtypeStruct((own.shape[0] // SHARE, rows, LANES), I16)]
        scratch = [pltpu.VMEM(own.shape, F32)] * 3
    else:
        outs = [shape, shape, shape, jax.ShapeDtypeStruct(codes.shape[1:], I16)]
        scratch = [pltpu.VMEM(own.shape, F32)]
        arguments.append(precond)
    in_specs = [SCALARS] + [WHOLE] * (len(arguments) - 1)
    return pl.pallas_call(
        lambda *refs: update_kernel(last, codes.shape[0], *refs),
        out_shape=outs,
        in_specs=in_specs,
        out_specs=[WHOLE] * len(outs),
        scratch_shapes=scratch,
        compiler_params=PARAMS,
        name="update",
    )(*arguments)


def finish_call(codes):
    shape = jax.ShapeDtypeStruct((SHARE, codes.shape[0] * COLS, LANES), F32)
    return pl.pallas_call(
        finish_kernel,
        out_shape=[shape, shape],
        in_specs=[WHOLE],
        out_specs=[WHOLE, WHOLE],
        compiler_params=PARAMS,
        name="finish",
    )(codes)


def local(right_side, diag_tiles, cond_tiles, neighbour_blocks, precision_diag, precond_tiles):
    depth, wide, high = (lax.axis_size(name) for name in ("z", "x", "y"))
    peers = wide * high
    here = right_side.shape[0]
    blocks = depth * here
    core = lax.axis_index("c")
    me = (lax.axis_index("x") * high + lax.axis_index("y")).astype(I32).reshape(1)
    half = here // 2

    own_diag = jnp.where(core == 0, diag_tiles[:half], diag_tiles[half:])
    mine = jnp.concatenate([cond_tiles.reshape(-1, LANES, LANES), own_diag], axis=0)
    tiles = lax.all_gather(mine, ("z", "c"), axis=0, tiled=False)
    tiles = tiles.reshape((depth, 2) + mine.shape)
    own_precond = lax.dynamic_slice_in_dim(precond_tiles, core * half, half, 0)

    wide_precond = precond_tiles.astype(F32)
    shaped = jnp.einsum("lts,lcs->lct", wide_precond, right_side, precision=lax.Precision.HIGHEST)
    near = jnp.pad(neighbour_blocks.astype(F32), ((0, 0), (0, LANES - neighbour_blocks.shape[1])))
    facts = jnp.concatenate([precision_diag, near], axis=0)
    facts = jnp.broadcast_to(facts[None], (depth,) + facts.shape)

    def by_column(values):
        values = values.reshape(here, depth, COLS, LANES).transpose(1, 0, 2, 3)
        return values.reshape(depth, here * COLS, LANES)

    sent = jnp.concatenate([by_column(right_side), by_column(shaped), facts], axis=1)
    came = lax.all_to_all(sent, "z", split_axis=0, concat_axis=0, tiled=True)
    rows = here * COLS
    residual = came[:, :rows].reshape(blocks, COLS, LANES)
    shaped = came[:, rows : 2 * rows].reshape(blocks, COLS, LANES)
    precision = came[:, 2 * rows : 2 * rows + here].reshape(blocks, LANES)
    near = came[:, 2 * rows + here :, : neighbour_blocks.shape[1]].astype(I32).reshape(-1)
    plane = near // (peers * here)
    near = (near // here) % peers * blocks + plane * here + near % here

    answer = jnp.zeros_like(residual)
    codes = start_call(shaped, residual)
    state = ()
    for iteration in range(ITERS):
        last = iteration + 1 == ITERS
        arrived = lax.all_gather(codes, ("x", "y"), axis=0, tiled=False)
        if iteration == 0:
            arrived, near, precision, tiles, own_precond = lax.optimization_barrier(
                (arrived, near, precision, tiles, own_precond)
            )
            precond = lax.all_gather(own_precond, ("z", "c"), axis=0, tiled=True)
        leaving, own, direction, gamma, *field = factor_call(
            iteration == 0, last, near, me, arrived, shaped, precision, tiles, state
        )
        terms = lax.all_to_all(leaving, ("x", "y"), split_axis=0, concat_axis=0, tiled=True)
        results = update_call(
            last, me, terms, own, residual, answer, direction, gamma, precond
        )
        if not last:
            residual, answer, shaped, codes = results
            state = (field[0], direction, gamma)

    codes = lax.all_to_all(results[0], "z", split_axis=0, concat_axis=0, tiled=True)
    answer, residual = finish_call(codes)
    return answer, residual


def solution(mesh, dims=DIMS):
    grid = Mesh(np.asarray(mesh.devices).reshape(dims + (2,)), ("z", "x", "y", "c"))
    blk = ("z", "x", "y")
    return jax.shard_map(
        local,
        mesh=grid,
        in_specs=(P(blk, "c", None), P(blk), P(blk, "c"), P(blk), P(blk), P(blk)),
        out_specs=(P(blk, "c", None), P(blk, "c", None)),
        check_vma=False,
    )
```
